128 devices in a mesh: dp: 4 (over x), fsdp: 32 (over z, y, core).
Axes of the slice: x: 4, y: 4, z: 4, core: 2. Of those that a mesh axis runs over, the one named last changes fastest.
Arguments:
- features: bfloat16 [49152, 3072], P(('dp', 'fsdp')), may hold values from -20 to 20
- cotangent: bfloat16 [49152, 3072], P(('dp', 'fsdp')), may hold values from -6 to 6
- weight: bfloat16 [3072, 3072], P('fsdp'), may hold values from -0.109375 to 0.109375
Outputs:
- sharp_grad: float32 [3072, 3072], P('fsdp')
The draws below stay inside these ranges and needn't reach their ends.
All inputs are finite; a program needn't handle non-finite values.
Results may differ from the reference program's by a relative error of at most 0.03.
Values may be sent and summed in bfloat16 or wider, within the bound.
A program may use at most 128 MiB of HBM per device.

```python
import jax
import jax.numpy as jnp
from jax import lax

DI = 3072
DO = 3072
TOK_DEV = 384
TOKENS = 49152


def draw_features(key, part):
    key = jax.random.fold_in(key, 7)
    key_base, key_rough = jax.random.split(key, 2)
    column = jnp.arange(DI, dtype=jnp.float32) / DI
    rough = jnp.exp(jax.random.uniform(key_rough, (DI,), minval=-0.35, maxval=0.35))
    scale = jnp.exp(jnp.log(3.0) * column) * rough * 0.6
    base = jnp.clip(jax.random.normal(key_base, (TOKENS, DI)), -5.0, 5.0)
    return (base * scale[None, :]).astype(jnp.bfloat16)


def shard_levels(key, shape, pieces, least, top_value):
    factor_of = 1.0
    for axis_at, blocks in pieces:
        steps = jax.random.uniform(jax.random.fold_in(jax.random.fold_in(key, 6), axis_at), (blocks,), jnp.float32, least / len(pieces), top_value / len(pieces))
        factor_of = factor_of * jnp.repeat(jnp.exp(steps), shape[axis_at] // blocks).reshape((-1,) + (1,) * (len(shape) - 1 - axis_at))
    return factor_of


def scatter_about(own_key, dims, scale, limit, pieces=(), kind=jnp.bfloat16):
    loudness = shard_levels(own_key, dims, pieces, -0.22, 0.18) if pieces else 1.0
    drawn = jax.random.normal(own_key, dims, jnp.float32) * scale * loudness
    return jnp.minimum(jnp.maximum(drawn, -limit), limit).astype(kind)


def setup_inputs(seed: int = 0) -> dict:
    keys = jax.random.split(jax.random.key(seed), 4)
    features = draw_features(jax.random.fold_in(keys[3], 71), 0)
    cotangent = scatter_about(keys[1], (TOKENS, DO), 1.0, 6.0, ((0, 128),))
    weight = scatter_about(keys[2], (DI, DO), DI ** -0.5, 0.109375, ((0, 32),))
    return {"features": features, "cotangent": cotangent, "weight": weight}


def gradient(features, cotangent, weight):
    act = jnp.dot(features, weight, preferred_element_type=jnp.float32)
    scaled = cotangent.astype(jnp.float32) / jnp.sqrt(jnp.float32(TOKENS))
    _, pull = jax.vjp(lambda v: jax.nn.gelu(v, approximate=True), act)
    delta = pull(scaled)[0].astype(jnp.bfloat16)
    blocks = TOKENS // TOK_DEV
    feat_blocks = features.reshape(blocks, TOK_DEV, DI)
    delta_blocks = delta.reshape(blocks, TOK_DEV, DO)

    def add_block(total, pair):
        feat_block, delta_block = pair
        term = jnp.dot(feat_block.T, delta_block, preferred_element_type=jnp.float32)
        term = lax.optimization_barrier(term.astype(jnp.bfloat16))
        return (total + term.astype(jnp.float32), None)
    total, _ = lax.scan(add_block, jnp.zeros((DI, DO), jnp.float32), (feat_blocks, delta_blocks))
    return total

def reference(features, cotangent, weight):
    first = gradient(features, cotangent, weight)
    norm = jnp.sqrt(jnp.sum(first * first) + 1e-06)
    radius = 0.3 * jnp.sqrt(jnp.float32(DO))
    perturbed = (weight.astype(jnp.float32) + radius * first / norm).astype(jnp.bfloat16)
    return gradient(features, cotangent, perturbed)
```

```python
import jax
import jax.numpy as jnp
from jax import lax
from jax.sharding import PartitionSpec as P


def make_delta(act, cotangent, total_tokens):
    scaled = cotangent.astype(jnp.float32) / jnp.sqrt(jnp.float32(total_tokens))
    _, pull = jax.vjp(lambda v: jax.nn.gelu(v, approximate=True), act)
    return pull(scaled)[0].astype(jnp.bfloat16)


def body(features, cotangent, weight):
    width = weight.shape[1]
    groups = lax.axis_size("dp")
    total_tokens = features.shape[0] * groups * lax.axis_size("fsdp")
    share = width // groups
    radius = 0.3 * jnp.sqrt(jnp.float32(width))

    mine = lax.dynamic_slice_in_dim(weight, lax.axis_index("dp") * share, share, 1)
    full = lax.all_gather(mine, "fsdp", axis=0, tiled=True)
    cot = lax.all_to_all(cotangent, "dp", split_axis=1, concat_axis=0, tiled=True)
    feats = lax.all_gather(features, "dp", axis=0, tiled=True)

    def grad(v):
        act = jnp.dot(feats, v, preferred_element_type=jnp.float32)
        delta = make_delta(act, cot, total_tokens)
        term = jnp.einsum("tr,tc->rc", feats, delta, preferred_element_type=jnp.float32)
        return lax.psum_scatter(
            term.astype(jnp.bfloat16), "fsdp", scatter_dimension=0, tiled=True
        )

    first = grad(full).astype(jnp.float32)
    squares = lax.psum(jnp.sum(first * first), ("dp", "fsdp"))
    norm = jnp.sqrt(squares + 1e-06)
    perturbed = (mine.astype(jnp.float32) + radius * first / norm).astype(jnp.bfloat16)
    second = grad(lax.all_gather(perturbed, "fsdp", axis=0, tiled=True))
    return lax.all_gather(second, "dp", axis=1, tiled=True).astype(jnp.float32)


def solution(mesh):
    in_specs = (P(("dp", "fsdp"), None), P(("dp", "fsdp"), None), P("fsdp", None))
    out_specs = P("fsdp", None)
    return jax.shard_map(body, mesh=mesh, in_specs=in_specs, out_specs=out_specs, check_vma=False)
```

```python
import jax
import jax.numpy as jnp
from jax import lax
from jax.experimental import pallas as pl
from jax.experimental.pallas import tpu as pltpu
from jax.sharding import PartitionSpec as P

MESH = pl.DeviceIdType.MESH
F32 = jnp.float32
BF16 = jnp.bfloat16

RING = 4
TOK = 384
DI = 3072
DO = 3072
ROWS = 96
BLK = 256
NB = 3
SHARE = BLK * NB
PART = 128
PARTS = TOK // PART
N_SEMS = 256
ROOT = 0.7978845608028654
CUBIC = 0.044715


def kernel(
    feat, cot, weight, out,
    f, ft, c, d, v1, v2, a1, a2, g, r1, r2, t, tx, o, nown, nrecv, kvec,
    send_sems, recv_sems, local_sems,
):
    x = lax.axis_index("dp")
    ff = lax.axis_index("fsdp")
    z = ff // 8
    y = lax.rem(ff // 2, RING)
    core = lax.rem(ff, 2)
    s = 1 - 2 * core

    def wrap(v):
        return lax.rem(v + 2 * RING, RING)

    def dev(dx=0, dy=0, dz=0, other=False):
        cc = 1 - core if other else core
        return (wrap(x + dx), (wrap(z + dz) * RING + wrap(y + dy)) * 2 + cc)

    def ring_dev(axis, step):
        return dev(dy=step) if axis == "y" else dev(dz=step)

    counter = [0]
    pending = []

    def remote(src, dst, device):
        i = counter[0]
        counter[0] += 1
        cp = pltpu.make_async_remote_copy(
            src_ref=src, dst_ref=dst, send_sem=send_sems.at[i], recv_sem=recv_sems.at[i],
            device_id=device, device_id_type=MESH,
        )
        cp.start()
        pending.append(cp)
        return cp

    def drain():
        while pending:
            pending.pop().wait_send()

    local_counter = [0]

    def local(src, dst):
        i = local_counter[0]
        local_counter[0] += 1
        cp = pltpu.make_async_copy(src, dst, local_sems.at[i])
        cp.start()
        return cp

    def columns(dx, other, j):
        cc = 1 - core if other else core
        start = (lax.rem(x + dx + RING, 2) * 2 + cc) * SHARE + j * BLK
        return pl.ds(pl.multiple_of(start, BLK), BLK)

    w_own = [local(weight.at[:, columns(0, False, j)], v1.at[j, z, y, core]) for j in range(NB)]
    f_own = local(feat, f.at[0])
    c_own = [local(cot.at[:, columns(0, False, j)], c.at[j, 0]) for j in range(NB)]

    barrier = pltpu.get_barrier_semaphore()
    others = [dev(other=True)]
    for step in (1, 2, 3):
        others += [dev(dx=step), dev(dx=step, other=True), dev(dy=step), dev(dz=step)]
    for other in others:
        pl.semaphore_signal(barrier, inc=1, device_id=other, device_id_type=MESH)
    pl.semaphore_wait(barrier, len(others))

    sib = dev(other=True)
    w_sib = [
        remote(weight.at[:, columns(0, True, j)], v1.at[j, z, y, core], sib) for j in range(NB)
    ]
    f_x = []
    for k in range(PARTS):
        rows = pl.ds(k * PART, PART)
        f_x.append(remote(feat.at[rows], f.at[2, rows], dev(dx=s)))
    f_sib = remote(feat, f.at[1], sib)
    c_sib, c_x, c_xo = [], [], []
    for j in range(NB):
        c_sib.append(remote(cot.at[:, columns(0, True, j)], c.at[j, 1], sib))
    for j in range(NB):
        c_x.append(remote(cot.at[:, columns(1, False, j)], c.at[j, 2], dev(dx=s)))
        c_xo.append(remote(cot.at[:, columns(1, True, j)], c.at[j, 3], dev(dx=s, other=True)))

    class Gather:
        def __init__(self, v, j):
            self.v, self.j = v, j

        def piece(self, half, stage, step):
            axis = self.axis(half, stage)
            zz = wrap(z + step) if axis == "z" else z
            yy = wrap(y + step) if axis == "y" else y
            if stage == 1:
                return self.v.at[self.j, zz, yy, half]
            if axis == "z":
                return self.v.at[self.j, zz, :, half]
            return self.v.at[self.j, :, yy, half]

        def axis(self, half, stage):
            return ("y", "z")[(half + stage + 1) % 2]

        def start(self, stage):
            self.near, self.far, self.relay = {}, {}, {}
            for half in (0, 1):
                axis, own = self.axis(half, stage), self.piece(half, stage, 0)
                self.near[half] = remote(own, own, ring_dev(axis, s))
                self.far[half] = remote(own, own, ring_dev(axis, -s))

        def forward(self, stage):
            for half in (0, 1):
                self.near[half].wait_recv()
                got = self.piece(half, stage, -s)
                self.relay[half] = remote(got, got, ring_dev(self.axis(half, stage), s))

        def finish(self, stage):
            for half in (0, 1):
                self.far[half].wait_recv()
                self.relay[half].wait_recv()

    class Scatter:
        def __init__(self, j):
            self.j = j

        def axis(self, half, stage):
            return ("z", "y")[(half + stage + 1) % 2]

        def place(self, half, stage, step):
            axis = self.axis(half, stage)
            zz = wrap(z + step) if axis == "z" else z
            yy = wrap(y + step) if axis == "y" else y
            if stage == 2:
                return (self.j, zz, yy, half)
            if axis == "z":
                return (self.j, zz, slice(None), half)
            return (self.j, slice(None), yy, half)

        def land(self, half, stage, i):
            return (r1 if stage == 1 else r2).at[self.j, half, i]

        def start(self, stage):
            self.first, self.back, self.merged = {}, {}, {}
            for half in (0, 1):
                axis = self.axis(half, stage)
                self.first[half] = remote(
                    g.at[self.place(half, stage, 2)], self.land(half, stage, 0), ring_dev(axis, s)
                )
                self.back[half] = remote(
                    g.at[self.place(half, stage, -s)], self.land(half, stage, 1), ring_dev(axis, -s)
                )

        def middle(self, stage):
            for half in (0, 1):
                self.first[half].wait_recv()
                at = self.place(half, stage, s)
                if stage == 1:
                    got = r1[self.j, half, 0]
                else:
                    got = r2[self.j, half, 0]
                g[at] = (g[at].astype(F32) + got.astype(F32)).astype(BF16)
                self.merged[half] = remote(
                    g.at[at], self.land(half, stage, 2), ring_dev(self.axis(half, stage), s)
                )

        def finish(self, stage):
            for half in (0, 1):
                self.back[half].wait_recv()
                self.merged[half].wait_recv()
                at = self.place(half, stage, 0)
                r = r1 if stage == 1 else r2
                total = g[at].astype(F32) + r[self.j, half, 1].astype(F32) + r[self.j, half, 2].astype(F32)
                if stage == 1:
                    g[at] = total.astype(BF16)
                else:
                    t[self.j, half] = total.astype(BF16)

    def transpose(slot, part):
        @pl.loop(0, DI // BLK)
        def _(i):
            cols = pl.ds(pl.multiple_of(i * BLK, BLK), BLK)
            ft[cols, pl.ds(slot * TOK + part * PART, PART)] = f[slot, pl.ds(part * PART, PART), cols].T

    def matmul(j, v, dst, slots):
        lo, hi = slots

        @pl.loop(lo, hi)
        def _(slot):
            dst[slot] = jnp.dot(f[slot], v[j].reshape(DI, BLK), preferred_element_type=F32)

    def act(j, slots):
        matmul(j, v1, a1.at[j], slots)

    def delta(j, slots, second):
        lo, hi = slots
        step = 64

        @pl.loop(lo * (TOK // step), hi * (TOK // step))
        def _(i):
            slot = i // (TOK // step)
            rows = pl.ds(pl.multiple_of(lax.rem(i, TOK // step) * step, step), step)
            a = a1[j, slot, rows, :]
            if second:
                a = a + a2[slot, rows, :] * kvec[0:1, :]
            square = a * a
            th = jnp.tanh(ROOT * a * (1.0 + CUBIC * square))
            slope = 0.5 * (1.0 + th) + 0.5 * a * (1.0 - th * th) * (ROOT * (1.0 + 3.0 * CUBIC * square))
            scaled = c[j, slot, rows, :].astype(F32) * (1.0 / jnp.sqrt(F32(TOK * 128)))
            d[j, slot, rows, :] = (scaled * slope).astype(BF16)

    def grad(j):
        rows = DI // RING

        @pl.loop(0, RING)
        def _(i):
            left = ft[pl.ds(pl.multiple_of(i * rows, rows), rows), :]
            term = jnp.dot(left, d[j].reshape(4 * TOK, BLK), preferred_element_type=F32)
            g[j, i] = term.astype(BF16).reshape(RING, 2, ROWS, BLK)

    ag = [Gather(v1, j) for j in range(NB)]
    for j in range(NB):
        w_own[j].wait()
        w_sib[j].wait_recv()
        ag[j].start(1)
    f_own.wait()
    for k in range(PARTS):
        transpose(0, k)
    for j in range(NB):
        ag[j].forward(1)
    for j in range(NB):
        ag[j].finish(1)
        ag[j].start(2)
    f_sib.wait_recv()
    for k in range(PARTS):
        transpose(1, k)

    f_fwd = []

    def take_part(k):
        rows = pl.ds(k * PART, PART)
        f_x[k].wait_recv()
        f_fwd.append(remote(f.at[2, rows], f.at[3, rows], sib))
        transpose(2, k)

    def take_forwarded(k):
        f_fwd[k].wait_recv()
        transpose(3, k)

    for cp in c_own:
        cp.wait()
    for cp in c_sib:
        cp.wait_recv()
    ag[0].forward(2)
    take_part(0)
    ag[0].finish(2)
    act(0, (0, 2))
    delta(0, (0, 2), False)
    ag[1].forward(2)
    take_forwarded(0)
    take_part(1)
    ag[1].finish(2)
    act(1, (0, 2))
    delta(1, (0, 2), False)
    ag[2].forward(2)
    take_forwarded(1)
    ag[2].finish(2)
    act(2, (0, 2))
    delta(2, (0, 2), False)
    take_part(2)
    take_forwarded(2)

    def rest(j):
        act(j, (2, 4))
        c_x[j].wait_recv()
        c_xo[j].wait_recv()
        delta(j, (2, 4), False)
        grad(j)

    rs = [Scatter(j) for j in range(NB)]
    rest(0)
    rs[0].start(1)
    rest(1)
    rs[0].middle(1)
    rs[1].start(1)
    rest(2)
    rs[0].finish(1)
    rs[0].start(2)
    rs[1].middle(1)
    rs[2].start(1)

    swap = {}

    def cross(j):
        rs[j].finish(2)
        swap[j] = remote(t.at[j], tx.at[j], dev(dx=2))

    def first(j, squares):
        swap[j].wait_recv()
        total = t[j].astype(F32) + tx[j].astype(F32)
        v2[j, z, y] = total.astype(BF16)
        sq = (total * total).reshape(2 * ROWS // 8, 8, BLK).sum(axis=0)
        return squares + sq[:, :128] + sq[:, 128:]

    ag = [Gather(v2, j) for j in range(NB)]
    squares = jnp.zeros((8, 128), F32)
    rs[0].middle(2)
    rs[1].finish(1)
    rs[1].start(2)
    rs[2].middle(1)
    cross(0)
    rs[1].middle(2)
    rs[2].finish(1)
    rs[2].start(2)
    squares = first(0, squares)
    ag[0].start(1)
    cross(1)
    rs[2].middle(2)
    ag[0].forward(1)
    squares = first(1, squares)
    ag[1].start(1)
    cross(2)
    ag[0].finish(1)
    ag[0].start(2)
    ag[1].forward(1)
    squares = first(2, squares)
    ag[2].start(1)

    def norm_send(i, value, devices):
        nown[i] = value
        return [remote(nown.at[i], nrecv.at[i, n], device) for n, device in enumerate(devices)]

    def norm_add(i, copies):
        total = nown[i]
        for n, cp in enumerate(copies):
            cp.wait_recv()
            total = total + nrecv[i, n]
        return total

    ns = norm_send(0, squares, [sib, dev(dx=1), dev(dx=1, other=True)])
    ag[1].finish(1)
    ag[1].start(2)
    ag[2].forward(1)
    ns = norm_send(1, norm_add(0, ns), [dev(dy=n) for n in (1, 2, 3)])
    ag[0].forward(2)
    ag[2].finish(1)
    ag[2].start(2)
    ns = norm_send(2, norm_add(1, ns), [dev(dz=n) for n in (1, 2, 3)])
    ag[0].finish(2)
    matmul(0, v2, a2, (0, 4))
    ag[1].forward(2)
    total = jnp.sum(norm_add(2, ns), keepdims=True)
    factor = 0.3 * jnp.sqrt(F32(DO)) / jnp.sqrt(total + 1e-06)
    kvec[...] = jnp.broadcast_to(factor, kvec.shape)

    drain()
    rs = [Scatter(j) for j in range(NB)]
    delta(0, (0, 4), True)
    grad(0)
    rs[0].start(1)
    ag[1].finish(2)
    matmul(1, v2, a2, (0, 4))
    ag[2].forward(2)
    delta(1, (0, 4), True)
    rs[0].middle(1)
    grad(1)
    rs[1].start(1)
    ag[2].finish(2)
    matmul(2, v2, a2, (0, 4))
    rs[0].finish(1)
    rs[0].start(2)
    rs[1].middle(1)
    delta(2, (0, 4), True)
    grad(2)
    rs[2].start(1)
    rs[0].middle(2)
    rs[1].finish(1)
    rs[1].start(2)
    rs[2].middle(1)

    share = {}

    def spread(j):
        rs[j].finish(2)
        share[j] = [remote(t.at[j, 1 - core], o.at[j, 0, 1], sib)]
        for step in (1, 2, 3):
            share[j].append(remote(t.at[j, core], o.at[j, step, 0], dev(dx=step)))
            share[j].append(remote(t.at[j, 1 - core], o.at[j, step, 1], dev(dx=step, other=True)))

    def collect(j):
        for cp in share[j]:
            cp.wait_recv()
        for other in (False, True):
            same = t[j, core] if not other else o[j, 0, 1]
            k = int(other)
            out[:, columns(0, other, j)] = same.astype(F32) + o[j, 2, k].astype(F32)
            out[:, columns(1, other, j)] = o[j, 1, k].astype(F32) + o[j, 3, k].astype(F32)

    spread(0)
    rs[1].middle(2)
    rs[2].finish(1)
    rs[2].start(2)
    spread(1)
    rs[2].middle(2)
    collect(0)
    spread(2)
    collect(1)
    collect(2)
    drain()


def body(features, cotangent, weight):
    return pl.pallas_call(
        kernel,
        out_shape=jax.ShapeDtypeStruct((ROWS, DO), F32),
        in_specs=[pl.BlockSpec(memory_space=pl.ANY)] * 3,
        out_specs=pl.BlockSpec(memory_space=pltpu.VMEM),
        scratch_shapes=[
            pltpu.VMEM((4, TOK, DI), BF16),
            pltpu.VMEM((DI, 4 * TOK), BF16),
            pltpu.VMEM((NB, 4, TOK, BLK), BF16),
            pltpu.VMEM((NB, 4, TOK, BLK), BF16),
            pltpu.VMEM((NB, RING, RING, 2, ROWS, BLK), BF16),
            pltpu.VMEM((NB, RING, RING, 2, ROWS, BLK), BF16),
            pltpu.VMEM((NB, 4, TOK, BLK), F32),
            pltpu.VMEM((4, TOK, BLK), F32),
            pltpu.VMEM((NB, RING, RING, 2, ROWS, BLK), BF16),
            pltpu.VMEM((NB, 2, 3, RING, ROWS, BLK), BF16),
            pltpu.VMEM((NB, 2, 3, ROWS, BLK), BF16),
            pltpu.VMEM((NB, 2, ROWS, BLK), BF16),
            pltpu.VMEM((NB, 2, ROWS, BLK), BF16),
            pltpu.VMEM((NB, 4, 2, ROWS, BLK), BF16),
            pltpu.VMEM((3, 8, 128), F32),
            pltpu.VMEM((3, 3, 8, 128), F32),
            pltpu.VMEM((8, BLK), F32),
            pltpu.SemaphoreType.DMA((N_SEMS,)),
            pltpu.SemaphoreType.DMA((N_SEMS,)),
            pltpu.SemaphoreType.DMA((8,)),
        ],
        compiler_params=pltpu.CompilerParams(
            collective_id=0, has_side_effects=True, vmem_limit_bytes=60 * 2**20
        ),
    )(features, cotangent, weight)


def solution(mesh):
    in_specs = (P(("dp", "fsdp"), None), P(("dp", "fsdp"), None), P("fsdp", None))
    out_specs = P("fsdp", None)
    return jax.shard_map(body, mesh=mesh, in_specs=in_specs, out_specs=out_specs, check_vma=False)
```

```python
import jax
import jax.numpy as jnp
from jax import lax
from jax.experimental import pallas as pl
from jax.experimental.pallas import tpu as pltpu
from jax.sharding import PartitionSpec as P

MESH = pl.DeviceIdType.MESH
F32 = jnp.float32
BF16 = jnp.bfloat16

RING = 4
TOK = 384
DI = 3072
DO = 3072
ROWS = 96
BLK = 256
NB = 3
SHARE = BLK * NB
PART = 128
PARTS = TOK // PART
N_SEMS = 256
ROOT = 0.7978845608028654
CUBIC = 0.044715
ORDER = (
    "aS0", "aS1", "aT0", "T1", "aT1", "F0", "aG0", "aS2", "G0", "aG1", "F1", "oA0", "oD0", "oG0", "aT2",
    "oA1", "oD1", "oG1", "G1", "F2", "aG2", "G2", "nA0", "nD0", "nG0", "rS0", "nA1", "nD1", "nG1", "rS1",
    "oA2", "oD2", "oG2", "rM0", "nA2", "nD2", "nG2", "rM1", "rT0", "rS2", "rT1", "rX0", "rM2", "rFirst0",
    "rX1", "bS0", "rT2", "rFirst1", "bT0", "bS1", "rX2", "bG0", "rFirst2", "N0", "bS2", "bT1", "N1", "pA0",
    "N2", "bT2", "pD0", "pG0", "bG1", "qS0", "bG2", "pA1", "qM0", "pD1", "pG1", "qS1", "pA2", "pD2", "qT0",
    "pG2", "qS2", "qM1", "qP0", "qC0", "qM2", "qT1", "qT2", "qP1", "qP2", "qC1", "qC2",
)


def kernel(
    feat, cot, weight, out,
    f, ft, c, d, v1, v2, a1, a2, g, r1, r2, t, tx, o, nown, nrecv, kvec,
    send_sems, recv_sems, local_sems,
):
    x = lax.axis_index("dp")
    ff = lax.axis_index("fsdp")
    z = ff // 8
    y = lax.rem(ff // 2, RING)
    core = lax.rem(ff, 2)
    s = 1 - 2 * core

    def wrap(v):
        return lax.rem(v + 2 * RING, RING)

    def dev(dx=0, dy=0, dz=0, other=False):
        cc = 1 - core if other else core
        return (wrap(x + dx), (wrap(z + dz) * RING + wrap(y + dy)) * 2 + cc)

    def ring_dev(axis, step):
        return dev(dy=step) if axis == "y" else dev(dz=step)

    counter = [0]
    pending = []

    def remote(src, dst, device):
        i = counter[0]
        counter[0] += 1
        cp = pltpu.make_async_remote_copy(
            src_ref=src, dst_ref=dst, send_sem=send_sems.at[i], recv_sem=recv_sems.at[i],
            device_id=device, device_id_type=MESH,
        )
        cp.start()
        pending.append(cp)
        return cp

    def drain():
        while pending:
            pending.pop().wait_send()

    def sent(copies):
        for cp in copies:
            cp.wait_send()
        pending[:] = [cp for cp in pending if not any(cp is other for other in copies)]

    local_counter = [0]

    def local(src, dst):
        i = local_counter[0]
        local_counter[0] += 1
        cp = pltpu.make_async_copy(src, dst, local_sems.at[i])
        cp.start()
        return cp

    def columns(dx, other, j):
        cc = 1 - core if other else core
        start = (lax.rem(x + dx + RING, 2) * 2 + cc) * SHARE + j * BLK
        return pl.ds(pl.multiple_of(start, BLK), BLK)

    def transpose(slot, part):
        @pl.loop(0, DI // BLK)
        def _(i):
            cols = pl.ds(pl.multiple_of(i * BLK, BLK), BLK)
            ft[cols, pl.ds(slot * TOK + part * PART, PART)] = f[slot, pl.ds(part * PART, PART), cols].T

    w_own = [local(weight.at[:, columns(0, False, j)], v1.at[j, z, y, core]) for j in range(NB)]
    f_own = local(feat, f.at[0])
    c_own = [local(cot.at[:, columns(0, False, j)], c.at[j, 0]) for j in range(NB)]

    barrier = pltpu.get_barrier_semaphore()
    norm_first = [dev(other=True), dev(dx=1), dev(dx=1, other=True)]
    norm_second = [dev(dy=n // RING, dz=n % RING) for n in range(1, RING * RING)]
    others = [dev(other=True)] + norm_second
    for step in (1, 2, 3):
        others += [dev(dx=step), dev(dx=step, other=True)]
    for other in others:
        pl.semaphore_signal(barrier, inc=1, device_id=other, device_id_type=MESH)
    f_own.wait()
    for k in range(PARTS):
        transpose(0, k)
    pl.semaphore_wait(barrier, len(others))

    sib = dev(other=True)
    w_sib = [
        remote(weight.at[:, columns(0, True, j)], v1.at[j, z, y, core], sib) for j in range(NB)
    ]
    f_x, c_x, c_xo = [], [], []

    def send_features(k):
        rows = pl.ds(k * PART, PART)
        f_x.append(remote(feat.at[rows], f.at[2, rows], dev(dx=s)))

    def send_cotangent(j):
        c_x.append(remote(cot.at[:, columns(1, False, j)], c.at[j, 2], dev(dx=s)))
        c_xo.append(remote(cot.at[:, columns(1, True, j)], c.at[j, 3], dev(dx=s, other=True)))

    for k in range(PARTS):
        send_features(k)
    for j in range(NB):
        send_cotangent(j)
    f_sib = remote(feat, f.at[1], sib)
    c_sib = [remote(cot.at[:, columns(0, True, j)], c.at[j, 1], sib) for j in range(NB)]

    class Gather:
        def __init__(self, v, j):
            self.v, self.j = v, j

        def piece(self, half, stage, step):
            axis = self.axis(half, stage)
            zz = wrap(z + step) if axis == "z" else z
            yy = wrap(y + step) if axis == "y" else y
            if stage == 1:
                return self.v.at[self.j, zz, yy, half]
            if axis == "z":
                return self.v.at[self.j, zz, :, half]
            return self.v.at[self.j, :, yy, half]

        def axis(self, half, stage):
            return ("y", "z")[(half + stage + 1) % 2]

        def start(self, stage):
            self.near, self.far, self.relay = {}, {}, {}
            self.direct = []
            for half in (0, 1):
                axis, own = self.axis(half, stage), self.piece(half, stage, 0)
                if stage == 1:
                    self.direct += [remote(own, own, ring_dev(axis, n)) for n in (1, 3, 2)]
                    continue
                self.near[half] = remote(own, own, ring_dev(axis, s))
                self.far[half] = remote(own, own, ring_dev(axis, -s))

        def forward(self, stage):
            for half in (0, 1):
                self.near[half].wait_recv()
                got = self.piece(half, stage, -s)
                self.relay[half] = remote(got, got, ring_dev(self.axis(half, stage), s))

        def finish(self, stage):
            for cp in self.direct:
                cp.wait_recv()
            for half in self.far:
                self.far[half].wait_recv()
                self.relay[half].wait_recv()

    class Scatter:
        def __init__(self, j):
            self.j = j
            self.first, self.back, self.merged, self.direct = {}, {}, {}, {}

        def axis(self, half, stage):
            return ("z", "y")[(half + stage + 1) % 2]

        def place(self, half, stage, step):
            axis = self.axis(half, stage)
            zz = wrap(z + step) if axis == "z" else z
            yy = wrap(y + step) if axis == "y" else y
            if stage == 2:
                return (self.j, zz, yy, half)
            if axis == "z":
                return (self.j, zz, slice(None), half)
            return (self.j, slice(None), yy, half)

        def land(self, half, stage, i):
            return (r1 if stage == 1 else r2).at[self.j, half, i]

        def copies(self):
            out = [cp for copies in self.direct.values() for cp in copies]
            return out + [*self.first.values(), *self.back.values(), *self.merged.values()]

        def start(self, stage):
            for half in (0, 1):
                axis = self.axis(half, stage)
                if stage == 2:
                    self.direct[half] = [
                        remote(
                            g.at[self.place(half, stage, n)], r2.at[self.j, half, n - 1], ring_dev(axis, n)
                        )
                        for n in (1, 3, 2)
                    ]
                    continue
                self.first[half] = remote(
                    g.at[self.place(half, stage, 2)], r1.at[self.j, half, 0], ring_dev(axis, s)
                )
                self.back[half] = remote(
                    g.at[self.place(half, stage, -s)], r1.at[self.j, half, 1], ring_dev(axis, -s)
                )

        def middle(self):
            for half in (0, 1):
                self.first[half].wait_recv()
                at = self.place(half, 1, s)
                g[at] = (g[at].astype(F32) + r1[self.j, half, 0].astype(F32)).astype(BF16)
                self.merged[half] = remote(
                    g.at[at], r1.at[self.j, half, 2], ring_dev(self.axis(half, 1), s)
                )

        def turn(self):
            for half in (0, 1):
                self.back[half].wait_recv()
                self.merged[half].wait_recv()
                at = self.place(half, 1, 0)
                total = g[at].astype(F32) + r1[self.j, half, 1].astype(F32) + r1[self.j, half, 2].astype(F32)
                g[at] = total.astype(BF16)
            self.start(2)

        def finish(self):
            for half in (0, 1):
                total = g[self.place(half, 2, 0)].astype(F32)
                for n, cp in enumerate(self.direct[half]):
                    cp.wait_recv()
                for n in range(3):
                    total = total + r2[self.j, half, n].astype(F32)
                t[self.j, half] = total.astype(BF16)

    def matmul(j, v, dst, lo, hi):
        product = jnp.dot(
            f[lo:hi].reshape((hi - lo) * TOK, DI), v[j].reshape(DI, BLK), preferred_element_type=F32
        )
        dst[lo:hi] = product.reshape(hi - lo, TOK, BLK)

    def delta(j, lo, hi, second):
        step = 64

        @pl.loop(lo, hi)
        def _(slot):
            @pl.loop(0, TOK // step)
            def _(i):
                rows = pl.ds(pl.multiple_of(i * step, step), step)
                a = a1[j, slot, rows, :]
                if second:
                    a = a + a2[slot, rows, :] * kvec[0:1, :]
                square = a * a
                th = jnp.tanh(ROOT * a * (1.0 + CUBIC * square))
                slope = 0.5 * (1.0 + th) + 0.5 * a * (1.0 - th * th) * (ROOT * (1.0 + 3.0 * CUBIC * square))
                scaled = c[j, slot, rows, :].astype(F32) * (1.0 / jnp.sqrt(F32(TOK * 128)))
                d[j, slot, rows, :] = (scaled * slope).astype(BF16)

    def grad(j, lo, hi, add):
        rows = DI // 2

        @pl.loop(0, 2)
        def _(i):
            left = ft[pl.ds(pl.multiple_of(i * rows, rows), rows), lo * TOK : hi * TOK]
            right = d[j, lo:hi].reshape((hi - lo) * TOK, BLK)
            term = jnp.dot(left, right, preferred_element_type=F32)
            at = (j, pl.ds(i * (RING // 2), RING // 2))
            if add:
                term = term + g[at].reshape(rows, BLK).astype(F32)
            g[at] = term.astype(BF16).reshape(RING // 2, RING, 2, ROWS, BLK)

    gather1 = [Gather(v1, j) for j in range(NB)]
    gather2 = [Gather(v2, j) for j in range(NB)]
    scatter1 = [Scatter(j) for j in range(NB)]
    scatter2 = [Scatter(j) for j in range(NB)]
    f_fwd, swap, share, state = {}, {}, {}, {}

    def weight_start(j):
        w_own[j].wait()
        w_sib[j].wait_recv()
        gather1[j].start(1)

    def gather_turn(ag):
        ag.finish(1)
        ag.start(2)

    def sibling_tokens():
        f_sib.wait_recv()
        for k in range(PARTS):
            transpose(1, k)

    def take_part(k):
        rows = pl.ds(k * PART, PART)
        f_x[k].wait_recv()
        f_fwd[k] = remote(f.at[2, rows], f.at[3, rows], sib)
        transpose(2, k)

    def take_forwarded(k):
        f_fwd[k].wait_recv()
        transpose(3, k)

    def own_act(j):
        gather1[j].finish(2)
        matmul(j, v1, a1.at[j], 0, 2)

    def own_delta(j):
        c_own[j].wait()
        c_sib[j].wait_recv()
        delta(j, 0, 2, False)

    def other_delta(j):
        c_x[j].wait_recv()
        c_xo[j].wait_recv()
        delta(j, 2, 4, False)

    def cross(j):
        scatter1[j].finish()
        swap[j] = remote(t.at[j], tx.at[j], dev(dx=2))

    def first(j):
        swap[j].wait_recv()
        total = t[j].astype(F32) + tx[j].astype(F32)
        v2[j, z, y] = total.astype(BF16)
        sq = (total * total).reshape(2 * ROWS // 8, 8, BLK).sum(axis=0)
        sq = sq[:, :128] + sq[:, 128:]
        nown[0] = sq if j == 0 else nown[0] + sq

    def norm_send(i, base, devices):
        state[i] = [remote(nown.at[i], nrecv.at[base + n], device) for n, device in enumerate(devices)]

    def norm_add(i, base):
        total = nown[i]
        for n, cp in enumerate(state[i]):
            cp.wait_recv()
            total = total + nrecv[base + n]
        return total

    def norm_start():
        norm_send(0, 0, norm_first)

    def norm_turn():
        nown[1] = norm_add(0, 0)
        norm_send(1, len(norm_first), norm_second)

    def norm_finish():
        total = jnp.sum(norm_add(1, len(norm_first)), keepdims=True)
        factor = 0.3 * jnp.sqrt(F32(DO)) / jnp.sqrt(total + 1e-06)
        kvec[...] = jnp.broadcast_to(factor, kvec.shape)

    def second_act(j):
        gather2[j].finish(2)
        matmul(j, v2, a2, 0, 4)

    def second_grad(j):
        sent(scatter1[j].copies())
        grad(j, 0, 4, False)

    def spread(j):
        sent([swap[j]])
        scatter2[j].finish()
        share[j] = [remote(t.at[j, 1 - core], o.at[j, 0, 1], sib)]
        for step in (2, 1, 3):
            share[j].append(remote(t.at[j, core], o.at[j, step, 0], dev(dx=step)))
            share[j].append(remote(t.at[j, 1 - core], o.at[j, step, 1], dev(dx=step, other=True)))

    def collect(j):
        for cp in share[j]:
            cp.wait_recv()
        for other in (False, True):
            same = t[j, core] if not other else o[j, 0, 1]
            k = int(other)
            out[:, columns(0, other, j)] = same.astype(F32) + o[j, 2, k].astype(F32)
            out[:, columns(1, other, j)] = o[j, 1, k].astype(F32) + o[j, 3, k].astype(F32)

    steps = {
        "aS": weight_start,
        "aT": lambda j: gather_turn(gather1[j]),
        "aG": lambda j: gather1[j].forward(2),
        "F": take_part,
        "G": take_forwarded,
        "oA": own_act,
        "oD": own_delta,
        "oG": lambda j: grad(j, 0, 2, False),
        "nA": lambda j: matmul(j, v1, a1.at[j], 2, 4),
        "nD": other_delta,
        "nG": lambda j: grad(j, 2, 4, True),
        "rS": lambda j: scatter1[j].start(1),
        "rM": lambda j: scatter1[j].middle(),
        "rT": lambda j: scatter1[j].turn(),
        "rX": cross,
        "rFirst": first,
        "bS": lambda j: gather2[j].start(1),
        "bT": lambda j: gather_turn(gather2[j]),
        "bG": lambda j: gather2[j].forward(2),
        "pA": second_act,
        "pD": lambda j: delta(j, 0, 4, True),
        "pG": second_grad,
        "qS": lambda j: scatter2[j].start(1),
        "qM": lambda j: scatter2[j].middle(),
        "qT": lambda j: scatter2[j].turn(),
        "qP": spread,
        "qC": collect,
    }
    single = {"T1": sibling_tokens, "N0": norm_start, "N1": norm_turn, "N2": norm_finish}
    for name in ORDER:
        if name in single:
            single[name]()
        else:
            steps[name[:-1]](int(name[-1]))
    drain()


def body(features, cotangent, weight):
    return pl.pallas_call(
        kernel,
        out_shape=jax.ShapeDtypeStruct((ROWS, DO), F32),
        in_specs=[pl.BlockSpec(memory_space=pl.ANY)] * 3,
        out_specs=pl.BlockSpec(memory_space=pltpu.VMEM),
        scratch_shapes=[
            pltpu.VMEM((4, TOK, DI), BF16),
            pltpu.VMEM((DI, 4 * TOK), BF16),
            pltpu.VMEM((NB, 4, TOK, BLK), BF16),
            pltpu.VMEM((NB, 4, TOK, BLK), BF16),
            pltpu.VMEM((NB, RING, RING, 2, ROWS, BLK), BF16),
            pltpu.VMEM((NB, RING, RING, 2, ROWS, BLK), BF16),
            pltpu.VMEM((NB, 4, TOK, BLK), F32),
            pltpu.VMEM((4, TOK, BLK), F32),
            pltpu.VMEM((NB, RING, RING, 2, ROWS, BLK), BF16),
            pltpu.VMEM((NB, 2, 3, RING, ROWS, BLK), BF16),
            pltpu.VMEM((NB, 2, 3, ROWS, BLK), BF16),
            pltpu.VMEM((NB, 2, ROWS, BLK), BF16),
            pltpu.VMEM((NB, 2, ROWS, BLK), BF16),
            pltpu.VMEM((NB, 4, 2, ROWS, BLK), BF16),
            pltpu.VMEM((2, 8, 128), F32),
            pltpu.VMEM((18, 8, 128), F32),
            pltpu.VMEM((8, BLK), F32),
            pltpu.SemaphoreType.DMA((N_SEMS,)),
            pltpu.SemaphoreType.DMA((N_SEMS,)),
            pltpu.SemaphoreType.DMA((8,)),
        ],
        compiler_params=pltpu.CompilerParams(
            collective_id=0, has_side_effects=True, vmem_limit_bytes=60 * 2**20
        ),
    )(features, cotangent, weight)


def solution(mesh):
    in_specs = (P(("dp", "fsdp"), None), P(("dp", "fsdp"), None), P("fsdp", None))
    out_specs = P("fsdp", None)
    return jax.shard_map(body, mesh=mesh, in_specs=in_specs, out_specs=out_specs, check_vma=False)
```

```python
import jax
import jax.numpy as jnp
from jax import lax
from jax.experimental import pallas as pl
from jax.experimental.pallas import tpu as pltpu
from jax.sharding import PartitionSpec as P

MESH = pl.DeviceIdType.MESH
F32 = jnp.float32
BF16 = jnp.bfloat16

RING = 4
TOK = 384
DI = 3072
DO = 3072
ROWS = 96
BLK = 256
NB = 3
SHARE = BLK * NB
PART = 128
PARTS = TOK // PART
N_SEMS = 45
LOW, HIGH = slice(0, RING // 2), slice(RING // 2, RING)
ROOT = 0.7978845608028654
CUBIC = 0.044715
ORDER = (
    "aS0", "aT0", "aS1", "T1", "aG0", "aS2", "F0", "G0", "aT1", "oA0", "oD0", "oG0", "F1", "aT2", "aG1", "G1",
    "aG2", "F2", "oA1", "G2", "nA0", "nD0", "nG0", "rS0", "nA1", "nD1", "oD1", "oG1", "rM0", "nG1", "rS1",
    "oA2", "oD2", "oG2", "rT0", "rM1", "nA2", "nD2", "nG2", "rS2", "rX0", "rT1", "rM2", "rFirst0", "bS0",
    "rX1", "rT2", "bT0", "rFirst1", "bS1", "rX2", "bG0", "rFirst2", "N0", "bS2", "bT1", "N1", "pA0", "N2",
    "pD0", "bT2", "pG0", "bG1", "qS0", "bG2", "pA1", "qM0", "pD1", "pG1", "qS1", "pA2", "qT0", "pD2", "pG2",
    "qS2", "qM1", "qP0", "qM2", "qC0", "qT1", "qT2", "qP1", "qP2", "qC1", "qC2",
)


def kernel(
    feat, cot, weight, out,
    f, ft, c, d, v1, v2, a1, a2, g, r1, r2, t, tx, o, nown, nrecv, kvec,
    send_sems, recv_sems, local_sems,
):
    x = lax.axis_index("dp")
    ff = lax.axis_index("fsdp")
    z = ff // 8
    y = lax.rem(ff // 2, RING)
    core = lax.rem(ff, 2)
    s = 1 - 2 * core

    def wrap(v):
        return lax.rem(v + 2 * RING, RING)

    def dev(dx=0, dy=0, dz=0, other=False):
        cc = 1 - core if other else core
        return (wrap(x + dx), (wrap(z + dz) * RING + wrap(y + dy)) * 2 + cc)

    def ring_dev(axis, step):
        return dev(dy=step) if axis == "y" else dev(dz=step)

    counter = [0]
    pending = []

    class Group:
        def __init__(self, like, again=None):
            self.like = like
            if again is None:
                self.i = counter[0]
                counter[0] += 1
            else:
                self.i = again.i

        def send(self, src, dst, device):
            if not any(group is self for group in pending):
                pending.append(self)
            pltpu.make_async_remote_copy(
                src_ref=src, dst_ref=dst, send_sem=send_sems.at[self.i], recv_sem=recv_sems.at[self.i],
                device_id=device, device_id_type=MESH,
            ).start()

        def wait_recv(self):
            pltpu.make_async_copy(self.like, self.like, recv_sems.at[self.i]).wait()

        def wait_send(self):
            pltpu.make_async_copy(self.like, self.like, send_sems.at[self.i]).wait()
            pending[:] = [group for group in pending if group is not self]

    def remote(src, dst, device):
        group = Group(dst)
        group.send(src, dst, device)
        return group

    def drain():
        for group in list(pending):
            group.wait_send()

    def sent(groups):
        for group in groups:
            group.wait_send()

    local_counter = [0]

    def local(src, dst):
        i = local_counter[0]
        local_counter[0] += 1
        cp = pltpu.make_async_copy(src, dst, local_sems.at[i])
        cp.start()
        return cp

    def columns(dx, other, j):
        cc = 1 - core if other else core
        start = (lax.rem(x + dx + RING, 2) * 2 + cc) * SHARE + j * BLK
        return pl.ds(pl.multiple_of(start, BLK), BLK)

    def transpose(slot, part):
        @pl.loop(0, DI // BLK)
        def _(i):
            cols = pl.ds(pl.multiple_of(i * BLK, BLK), BLK)
            ft[cols, pl.ds(slot * TOK + part * PART, PART)] = f[slot, pl.ds(part * PART, PART), cols].T

    barrier = pltpu.get_barrier_semaphore()
    norm_first = [dev(other=True), dev(dx=1), dev(dx=1, other=True)]
    norm_second = [dev(dy=n // RING, dz=n % RING) for n in range(1, RING * RING)]
    others = [dev(other=True)] + norm_second
    for step in (1, 2, 3):
        others += [dev(dx=step), dev(dx=step, other=True)]
    for other in others:
        pl.semaphore_signal(barrier, inc=1, device_id=other, device_id_type=MESH)
    w_own = [local(weight.at[:, columns(0, False, j)], v1.at[j, z, y, core]) for j in range(NB)]
    f_own = local(feat, f.at[0])
    c_own = [local(cot.at[:, columns(0, False, j)], c.at[j, 0]) for j in range(NB)]
    pl.semaphore_wait(barrier, len(others))

    sib = dev(other=True)
    f_x, c_x = [], []

    def send_features(k):
        rows = pl.ds(k * PART, PART)
        f_x.append(remote(feat.at[rows], f.at[2, rows], dev(dx=s)))

    def send_cotangent(j):
        c_x.append(Group(c.at[j, 2:4]))
        c_x[j].send(cot.at[:, columns(1, False, j)], c.at[j, 2], dev(dx=s))
        c_x[j].send(cot.at[:, columns(1, True, j)], c.at[j, 3], dev(dx=s, other=True))

    for k in range(PARTS):
        send_features(k)
    for j in range(NB):
        send_cotangent(j)
    w_sib = [
        remote(weight.at[:, columns(0, True, j)], v1.at[j, z, y, core], sib) for j in range(NB)
    ]
    f_sib = remote(feat, f.at[1], sib)
    c_sib = [remote(cot.at[:, columns(0, True, j)], c.at[j, 1], sib) for j in range(NB)]

    f_own.wait()
    for k in range(PARTS):
        transpose(0, k)

    class Gather:
        def __init__(self, v, j, again=None):
            self.v, self.j = v, j
            likes = (v.at[j, 0, 0:3], v.at[j, 0], v.at[j, 0:2])
            self.groups = [Group(like, again and again.groups[i]) for i, like in enumerate(likes)]
            self.direct, self.early, self.late = self.groups

        def axis(self, half, stage):
            return ("y", "z")[(half + stage + 1) % 2]

        def piece(self, half, stage, step, part=None):
            axis = self.axis(half, stage)
            zz = wrap(z + step) if axis == "z" else z
            yy = wrap(y + step) if axis == "y" else y
            if stage == 1:
                return self.v.at[self.j, zz, yy, half]
            if axis == "z":
                return self.v.at[self.j, zz, part, half]
            return self.v.at[self.j, part, yy, half]

        def start(self):
            for half in (0, 1):
                own, axis = self.piece(half, 1, 0), self.axis(half, 1)
                for n in (1, 3, 2):
                    self.direct.send(own, own, ring_dev(axis, n))

        def turn(self):
            self.direct.wait_recv()
            for group, parts in ((self.early, (LOW, HIGH)), (self.late, (HIGH, LOW))):
                for step, part in zip((1, -1), parts):
                    for half in (0, 1):
                        own = self.piece(half, 2, 0, part)
                        group.send(own, own, ring_dev(self.axis(half, 2), step))

        def forward(self):
            self.early.wait_recv()
            for step, part in ((1, LOW), (-1, HIGH)):
                for half in (0, 1):
                    got = self.piece(half, 2, -step, part)
                    self.late.send(got, got, ring_dev(self.axis(half, 2), step))

        def finish(self):
            self.late.wait_recv()

    class Scatter:
        def __init__(self, j, again=None):
            self.j = j
            likes = (r1.at[j, :, 0], r1.at[j, :, 1:3], r2.at[j])
            self.groups = [Group(like, again and again.groups[i]) for i, like in enumerate(likes)]
            self.far, self.near, self.direct = self.groups

        def axis(self, half, stage):
            return ("z", "y")[(half + stage + 1) % 2]

        def place(self, half, stage, step, part=slice(None)):
            axis = self.axis(half, stage)
            zz = wrap(z + step) if axis == "z" else z
            yy = wrap(y + step) if axis == "y" else y
            if stage == 2:
                return (self.j, zz, yy, half)
            if axis == "z":
                return (self.j, zz, part, half)
            return (self.j, part, yy, half)

        def send(self, group, half, step, to, part, land):
            group.send(
                g.at[self.place(half, 1, step, part)], r1.at[self.j, half, land, part], ring_dev(self.axis(half, 1), to)
            )

        def start(self):
            for step, part in ((1, LOW), (-1, HIGH)):
                for half in (0, 1):
                    self.send(self.far, half, 2, step, part, 0)
            for step, part, land in ((1, HIGH, 1), (-1, LOW, 2)):
                for half in (0, 1):
                    self.send(self.near, half, step, step, part, land)

        def middle(self):
            self.far.wait_recv()
            for step, part, land in ((1, LOW, 1), (-1, HIGH, 2)):
                for half in (0, 1):
                    at = self.place(half, 1, step, part)
                    g[at] = (g[at].astype(F32) + r1[self.j, half, 0, part].astype(F32)).astype(BF16)
                    self.send(self.near, half, step, step, part, land)

        def turn(self):
            self.near.wait_recv()
            for half in (0, 1):
                at = self.place(half, 1, 0)
                total = g[at].astype(F32) + r1[self.j, half, 1].astype(F32) + r1[self.j, half, 2].astype(F32)
                g[at] = total.astype(BF16)
                for n in (1, 3, 2):
                    self.direct.send(
                        g.at[self.place(half, 2, n)], r2.at[self.j, half, n - 1], ring_dev(self.axis(half, 2), n)
                    )

        def finish(self):
            self.direct.wait_recv()
            for half in (0, 1):
                total = g[self.place(half, 2, 0)].astype(F32)
                for n in range(3):
                    total = total + r2[self.j, half, n].astype(F32)
                t[self.j, half] = total.astype(BF16)

    def matmul(j, v, dst, lo, hi):
        @pl.loop(lo, hi)
        def _(slot):
            dst[slot] = jnp.dot(f[slot], v[j].reshape(DI, BLK), preferred_element_type=F32)

    def delta(j, lo, hi, second):
        step = 64

        @pl.loop(lo, hi)
        def _(slot):
            @pl.loop(0, TOK // step)
            def _(i):
                rows = pl.ds(pl.multiple_of(i * step, step), step)
                a = a1[j, slot, rows, :]
                if second:
                    a = a + a2[slot, rows, :] * kvec[0:1, :]
                square = a * a
                th = jnp.tanh(ROOT * a * (1.0 + CUBIC * square))
                slope = 0.5 * (1.0 + th) + 0.5 * a * (1.0 - th * th) * (ROOT * (1.0 + 3.0 * CUBIC * square))
                scaled = c[j, slot, rows, :].astype(F32) * (1.0 / jnp.sqrt(F32(TOK * 128)))
                d[j, slot, rows, :] = (scaled * slope).astype(BF16)

    def grad(j, lo, hi, add):
        rows = DI // 4

        @pl.loop(0, 4)
        def _(i):
            left = ft[pl.ds(pl.multiple_of(i * rows, rows), rows), lo * TOK : hi * TOK]
            right = d[j, lo:hi].reshape((hi - lo) * TOK, BLK)
            term = jnp.dot(left, right, preferred_element_type=F32)
            at = (j, pl.ds(i, 1))
            if add:
                term = term + g[at].reshape(rows, BLK).astype(F32)
            g[at] = term.astype(BF16).reshape(1, RING, 2, ROWS, BLK)

    gather1 = [Gather(v1, j) for j in range(NB)]
    gather2 = [Gather(v2, j, gather1[j]) for j in range(NB)]
    scatter1 = [Scatter(j) for j in range(NB)]
    scatter2 = [Scatter(j, scatter1[j]) for j in range(NB)]
    f_fwd, swap, share, state = {}, {}, {}, {}

    def weight_start(j):
        w_own[j].wait()
        w_sib[j].wait_recv()
        gather1[j].start()

    def sibling_tokens():
        f_sib.wait_recv()
        for k in range(PARTS):
            transpose(1, k)

    def take_part(k):
        rows = pl.ds(k * PART, PART)
        f_x[k].wait_recv()
        f_fwd[k] = remote(f.at[2, rows], f.at[3, rows], sib)
        transpose(2, k)

    def take_forwarded(k):
        f_fwd[k].wait_recv()
        transpose(3, k)

    def own_act(j):
        gather1[j].finish()
        matmul(j, v1, a1.at[j], 0, 2)

    def own_delta(j):
        c_own[j].wait()
        c_sib[j].wait_recv()
        delta(j, 0, 2, False)

    def other_delta(j):
        c_x[j].wait_recv()
        delta(j, 2, 4, False)

    def gather_start(j):
        sent(gather1[j].groups)
        gather2[j].start()

    def cross(j):
        scatter1[j].finish()
        swap[j] = remote(t.at[j], tx.at[j], dev(dx=2))

    def first(j):
        swap[j].wait_recv()
        total = t[j].astype(F32) + tx[j].astype(F32)
        v2[j, z, y] = total.astype(BF16)
        sq = (total * total).reshape(2 * ROWS // 8, 8, BLK).sum(axis=0)
        sq = sq[:, :128] + sq[:, 128:]
        nown[0] = sq if j == 0 else nown[0] + sq

    def norm_send(i, base, devices):
        state[i] = Group(nrecv.at[base : base + len(devices)])
        for n, device in enumerate(devices):
            state[i].send(nown.at[i], nrecv.at[base + n], device)

    def norm_add(i, base, count):
        state[i].wait_recv()
        return nown[i] + nrecv[base : base + count].sum(axis=0)

    def norm_start():
        norm_send(0, 0, norm_first)

    def norm_turn():
        nown[1] = norm_add(0, 0, len(norm_first))
        norm_send(1, len(norm_first), norm_second)

    def norm_finish():
        total = jnp.sum(norm_add(1, len(norm_first), len(norm_second)), keepdims=True)
        factor = 0.3 * jnp.sqrt(F32(DO)) / jnp.sqrt(total + 1e-06)
        kvec[...] = jnp.broadcast_to(factor, kvec.shape)

    def second_act(j):
        gather2[j].finish()
        matmul(j, v2, a2, 0, 4)

    def second_grad(j):
        sent(scatter1[j].groups)
        grad(j, 0, 4, False)

    def spread(j):
        sent([swap[j]])
        scatter2[j].finish()
        far = Group(o.at[j, 1:4])
        for step in (2, 1, 3):
            far.send(t.at[j, core], o.at[j, step, 0], dev(dx=step))
            far.send(t.at[j, 1 - core], o.at[j, step, 1], dev(dx=step, other=True))
        share[j] = [far, remote(t.at[j, 1 - core], o.at[j, 0, 1], sib)]

    def collect(j):
        for cp in share[j]:
            cp.wait_recv()
        for other in (False, True):
            same = t[j, core] if not other else o[j, 0, 1]
            k = int(other)
            out[:, columns(0, other, j)] = same.astype(F32) + o[j, 2, k].astype(F32)
            out[:, columns(1, other, j)] = o[j, 1, k].astype(F32) + o[j, 3, k].astype(F32)

    steps = {
        "aS": weight_start,
        "aT": lambda j: gather1[j].turn(),
        "aG": lambda j: gather1[j].forward(),
        "F": take_part,
        "G": take_forwarded,
        "oA": own_act,
        "oD": own_delta,
        "oG": lambda j: grad(j, 0, 2, False),
        "nA": lambda j: matmul(j, v1, a1.at[j], 2, 4),
        "nD": other_delta,
        "nG": lambda j: grad(j, 2, 4, True),
        "rS": lambda j: scatter1[j].start(),
        "rM": lambda j: scatter1[j].middle(),
        "rT": lambda j: scatter1[j].turn(),
        "rX": cross,
        "rFirst": first,
        "bS": gather_start,
        "bT": lambda j: gather2[j].turn(),
        "bG": lambda j: gather2[j].forward(),
        "pA": second_act,
        "pD": lambda j: delta(j, 0, 4, True),
        "pG": second_grad,
        "qS": lambda j: scatter2[j].start(),
        "qM": lambda j: scatter2[j].middle(),
        "qT": lambda j: scatter2[j].turn(),
        "qP": spread,
        "qC": collect,
    }
    single = {"T1": sibling_tokens, "N0": norm_start, "N1": norm_turn, "N2": norm_finish}
    for name in ORDER:
        if name in single:
            single[name]()
        else:
            steps[name[:-1]](int(name[-1]))
    drain()


def body(features, cotangent, weight):
    return pl.pallas_call(
        kernel,
        out_shape=jax.ShapeDtypeStruct((ROWS, DO), F32),
        in_specs=[pl.BlockSpec(memory_space=pl.ANY)] * 3,
        out_specs=pl.BlockSpec(memory_space=pltpu.VMEM),
        scratch_shapes=[
            pltpu.VMEM((4, TOK, DI), BF16),
            pltpu.VMEM((DI, 4 * TOK), BF16),
            pltpu.VMEM((NB, 4, TOK, BLK), BF16),
            pltpu.VMEM((NB, 4, TOK, BLK), BF16),
            pltpu.VMEM((NB, RING, RING, 2, ROWS, BLK), BF16),
            pltpu.VMEM((NB, RING, RING, 2, ROWS, BLK), BF16),
            pltpu.VMEM((NB, 4, TOK, BLK), F32),
            pltpu.VMEM((4, TOK, BLK), F32),
            pltpu.VMEM((NB, RING, RING, 2, ROWS, BLK), BF16),
            pltpu.VMEM((NB, 2, 3, RING, ROWS, BLK), BF16),
            pltpu.VMEM((NB, 2, 3, ROWS, BLK), BF16),
            pltpu.VMEM((NB, 2, ROWS, BLK), BF16),
            pltpu.VMEM((NB, 2, ROWS, BLK), BF16),
            pltpu.VMEM((NB, 4, 2, ROWS, BLK), BF16),
            pltpu.VMEM((2, 8, 128), F32),
            pltpu.VMEM((18, 8, 128), F32),
            pltpu.VMEM((8, BLK), F32),
            pltpu.SemaphoreType.DMA((N_SEMS,)),
            pltpu.SemaphoreType.DMA((N_SEMS,)),
            pltpu.SemaphoreType.DMA((8,)),
        ],
        compiler_params=pltpu.CompilerParams(
            collective_id=0, has_side_effects=True, vmem_limit_bytes=60 * 2**20
        ),
    )(features, cotangent, weight)


def solution(mesh):
    in_specs = (P(("dp", "fsdp"), None), P(("dp", "fsdp"), None), P("fsdp", None))
    out_specs = P("fsdp", None)
    return jax.shard_map(body, mesh=mesh, in_specs=in_specs, out_specs=out_specs, check_vma=False)
```

```python
import jax
import jax.numpy as jnp
from jax import lax
from jax.experimental import pallas as pl
from jax.experimental.pallas import tpu as pltpu
from jax.sharding import PartitionSpec as P

MESH = pl.DeviceIdType.MESH
F32 = jnp.float32
BF16 = jnp.bfloat16

RING = 4
TOK = 384
DI = 3072
DO = 3072
ROWS = 96
BLK = 256
NB = 3
SHARE = BLK * NB
PART = 128
PARTS = TOK // PART
N_SEMS = 46
LOW, HIGH = slice(0, RING // 2), slice(RING // 2, RING)
ROOT = 0.7978845608028654
CUBIC = 0.044715
ORDER = (
    "aS0", "aT0", "aS1", "T1", "aG0", "aS2", "F0", "G0", "aT1", "oA0", "oD0", "oG0", "F1", "aT2", "aG1", "G1",
    "aG2", "F2", "G2", "nA0", "nD0", "nG0", "rS0", "oA1", "oD1", "oG1", "nA1", "nD1", "rM0", "nG1", "rS1",
    "oA2", "oD2", "oG2", "rT0", "rM1", "nA2", "nD2", "nG2", "rS2", "rX0", "rT1", "rM2", "rFirst0", "bS0",
    "rX1", "rT2", "bT0", "rFirst1", "bS1", "rX2", "bG0", "rFirst2", "N0", "bS2", "N1", "bT1", "N2", "pA0",
    "N3", "bT2", "pD0", "pG0", "bG1", "qS0", "bG2", "pA1", "qM0", "pD1", "pG1", "qS1", "pA2", "qT0", "pD2",
    "pG2", "qS2", "qM1", "qP0", "qM2", "qC0", "qT1", "qT2", "qP1", "qP2", "qC1", "qC2",
)


def kernel(
    feat, cot, weight, out,
    f, ft, c, d, v1, v2, a1, a2, g, r1, r2, t, tx, o, nown, nrecv, kvec, result,
    send_sems, recv_sems, local_sems,
):
    x = lax.axis_index("dp")
    ff = lax.axis_index("fsdp")
    z = ff // 8
    y = lax.rem(ff // 2, RING)
    core = lax.rem(ff, 2)
    s = 1 - 2 * core

    def wrap(v):
        return lax.rem(v + 2 * RING, RING)

    def dev(dx=0, dy=0, dz=0, other=False):
        cc = 1 - core if other else core
        return (wrap(x + dx), (wrap(z + dz) * RING + wrap(y + dy)) * 2 + cc)

    def ring_dev(axis, step):
        return dev(dy=step) if axis == "y" else dev(dz=step)

    counter = [0]
    pending = []

    class Group:
        def __init__(self, like, again=None):
            self.like = like
            if again is None:
                self.i = counter[0]
                counter[0] += 1
            else:
                self.i = again.i

        def send(self, src, dst, device):
            if not any(group is self for group in pending):
                pending.append(self)
            pltpu.make_async_remote_copy(
                src_ref=src, dst_ref=dst, send_sem=send_sems.at[self.i], recv_sem=recv_sems.at[self.i],
                device_id=device, device_id_type=MESH,
            ).start()

        def wait_recv(self):
            pltpu.make_async_copy(self.like, self.like, recv_sems.at[self.i]).wait()

        def wait_send(self):
            pltpu.make_async_copy(self.like, self.like, send_sems.at[self.i]).wait()
            pending[:] = [group for group in pending if group is not self]

    def remote(src, dst, device):
        group = Group(dst)
        group.send(src, dst, device)
        return group

    def drain():
        for group in list(pending):
            group.wait_send()

    def sent(groups):
        for group in groups:
            group.wait_send()

    local_counter = [0]

    def local(src, dst):
        i = local_counter[0]
        local_counter[0] += 1
        cp = pltpu.make_async_copy(src, dst, local_sems.at[i])
        cp.start()
        return cp

    def columns(dx, other, j):
        cc = 1 - core if other else core
        start = (lax.rem(x + dx + RING, 2) * 2 + cc) * SHARE + j * BLK
        return pl.ds(pl.multiple_of(start, BLK), BLK)

    def transpose(slot, part):
        @pl.loop(0, DI // BLK)
        def _(i):
            cols = pl.ds(pl.multiple_of(i * BLK, BLK), BLK)
            ft[cols, pl.ds(slot * TOK + part * PART, PART)] = f[slot, pl.ds(part * PART, PART), cols].T

    barrier = pltpu.get_barrier_semaphore()
    norm_first = [dev(other=True), dev(dx=1), dev(dx=1, other=True)]
    norm_rings = (norm_first, [dev(dy=n) for n in (1, 2, 3)], [dev(dz=n) for n in (1, 2, 3)])
    others = [dev(other=True)]
    for step in (1, 2, 3):
        others += [dev(dx=step), dev(dx=step, other=True), dev(dy=step), dev(dz=step)]
    for other in others:
        pl.semaphore_signal(barrier, inc=1, device_id=other, device_id_type=MESH)
    w_own = [local(weight.at[:, columns(0, False, j)], v1.at[j, z, y, core]) for j in range(NB)]
    f_own = local(feat, f.at[0])
    c_own = [local(cot.at[:, columns(0, False, j)], c.at[j, 0]) for j in range(NB)]
    pl.semaphore_wait(barrier, len(others))

    sib = dev(other=True)
    f_x, c_x = [], []

    def send_features(k):
        rows = pl.ds(k * PART, PART)
        f_x.append(remote(feat.at[rows], f.at[2, rows], dev(dx=s)))

    def send_cotangent(j):
        c_x.append(Group(c.at[j, 2:4]))
        c_x[j].send(cot.at[:, columns(1, False, j)], c.at[j, 2], dev(dx=s))
        c_x[j].send(cot.at[:, columns(1, True, j)], c.at[j, 3], dev(dx=s, other=True))

    for k in range(PARTS):
        send_features(k)
    for j in range(NB):
        send_cotangent(j)
    w_sib = [
        remote(weight.at[:, columns(0, True, j)], v1.at[j, z, y, core], sib) for j in range(NB)
    ]
    f_sib = remote(feat, f.at[1], sib)
    c_sib = [remote(cot.at[:, columns(0, True, j)], c.at[j, 1], sib) for j in range(NB)]

    f_own.wait()
    for k in range(PARTS):
        transpose(0, k)

    class Gather:
        def __init__(self, v, j, again=None):
            self.v, self.j = v, j
            likes = (v.at[j, 0, 0:3], v.at[j, 0], v.at[j, 0:2])
            self.groups = [Group(like, again and again.groups[i]) for i, like in enumerate(likes)]
            self.direct, self.early, self.late = self.groups

        def axis(self, half, stage):
            return ("y", "z")[(half + stage + 1) % 2]

        def piece(self, half, stage, step, part=None):
            axis = self.axis(half, stage)
            zz = wrap(z + step) if axis == "z" else z
            yy = wrap(y + step) if axis == "y" else y
            if stage == 1:
                return self.v.at[self.j, zz, yy, half]
            if axis == "z":
                return self.v.at[self.j, zz, part, half]
            return self.v.at[self.j, part, yy, half]

        def start(self):
            for half in (0, 1):
                own, axis = self.piece(half, 1, 0), self.axis(half, 1)
                for n in (1, 3, 2):
                    self.direct.send(own, own, ring_dev(axis, n))

        def turn(self):
            self.direct.wait_recv()
            for group, parts in ((self.early, (LOW, HIGH)), (self.late, (HIGH, LOW))):
                for step, part in zip((1, -1), parts):
                    for half in (0, 1):
                        own = self.piece(half, 2, 0, part)
                        group.send(own, own, ring_dev(self.axis(half, 2), step))

        def forward(self):
            self.early.wait_recv()
            for step, part in ((1, LOW), (-1, HIGH)):
                for half in (0, 1):
                    got = self.piece(half, 2, -step, part)
                    self.late.send(got, got, ring_dev(self.axis(half, 2), step))

        def finish(self):
            self.late.wait_recv()

    class Scatter:
        def __init__(self, j, again=None):
            self.j = j
            likes = (r1.at[j, :, 0], r1.at[j, :, 1:3], r2.at[j])
            self.groups = [Group(like, again and again.groups[i]) for i, like in enumerate(likes)]
            self.far, self.near, self.direct = self.groups

        def axis(self, half, stage):
            return ("z", "y")[(half + stage + 1) % 2]

        def place(self, half, stage, step, part=slice(None)):
            axis = self.axis(half, stage)
            zz = wrap(z + step) if axis == "z" else z
            yy = wrap(y + step) if axis == "y" else y
            if stage == 2:
                return (self.j, zz, yy, half)
            if axis == "z":
                return (self.j, zz, part, half)
            return (self.j, part, yy, half)

        def send(self, group, half, step, to, part, land):
            group.send(
                g.at[self.place(half, 1, step, part)], r1.at[self.j, half, land, part], ring_dev(self.axis(half, 1), to)
            )

        def start(self):
            for step, part in ((1, LOW), (-1, HIGH)):
                for half in (0, 1):
                    self.send(self.far, half, 2, step, part, 0)
            for step, part, land in ((1, HIGH, 1), (-1, LOW, 2)):
                for half in (0, 1):
                    self.send(self.near, half, step, step, part, land)

        def middle(self):
            self.far.wait_recv()
            for step, part, land in ((1, LOW, 1), (-1, HIGH, 2)):
                for half in (0, 1):
                    at = self.place(half, 1, step, part)
                    g[at] = (g[at].astype(F32) + r1[self.j, half, 0, part].astype(F32)).astype(BF16)
                    self.send(self.near, half, step, step, part, land)

        def turn(self):
            self.near.wait_recv()
            for half in (0, 1):
                at = self.place(half, 1, 0)
                total = g[at].astype(F32) + r1[self.j, half, 1].astype(F32) + r1[self.j, half, 2].astype(F32)
                g[at] = total.astype(BF16)
                for n in (1, 3, 2):
                    self.direct.send(
                        g.at[self.place(half, 2, n)], r2.at[self.j, half, n - 1], ring_dev(self.axis(half, 2), n)
                    )

        def finish(self):
            self.direct.wait_recv()
            for half in (0, 1):
                total = g[self.place(half, 2, 0)].astype(F32)
                for n in range(3):
                    total = total + r2[self.j, half, n].astype(F32)
                t[self.j, half] = total.astype(BF16)

    def matmul(j, v, dst, lo, hi):
        @pl.loop(lo, hi)
        def _(slot):
            dst[slot] = jnp.dot(f[slot], v[j].reshape(DI, BLK), preferred_element_type=F32)

    def delta(j, lo, hi, second):
        step = 64

        @pl.loop(lo, hi)
        def _(slot):
            @pl.loop(0, TOK // step)
            def _(i):
                rows = pl.ds(pl.multiple_of(i * step, step), step)
                a = a1[j, slot, rows, :]
                if second:
                    a = a + a2[slot, rows, :] * kvec[0:1, :]
                square = a * a
                th = jnp.tanh(ROOT * a * (1.0 + CUBIC * square))
                slope = 0.5 * (1.0 + th) + 0.5 * a * (1.0 - th * th) * (ROOT * (1.0 + 3.0 * CUBIC * square))
                scaled = c[j, slot, rows, :].astype(F32) * (1.0 / jnp.sqrt(F32(TOK * 128)))
                d[j, slot, rows, :] = (scaled * slope).astype(BF16)

    def grad(j, lo, hi, add):
        rows = DI // 4

        @pl.loop(0, 4)
        def _(i):
            left = ft[pl.ds(pl.multiple_of(i * rows, rows), rows), lo * TOK : hi * TOK]
            right = d[j, lo:hi].reshape((hi - lo) * TOK, BLK)
            term = jnp.dot(left, right, preferred_element_type=F32)
            at = (j, pl.ds(i, 1))
            if add:
                term = term + g[at].reshape(rows, BLK).astype(F32)
            g[at] = term.astype(BF16).reshape(1, RING, 2, ROWS, BLK)

    gather1 = [Gather(v1, j) for j in range(NB)]
    gather2 = [Gather(v2, j, gather1[j]) for j in range(NB)]
    scatter1 = [Scatter(j) for j in range(NB)]
    scatter2 = [Scatter(j, scatter1[j]) for j in range(NB)]
    f_fwd, swap, share, state = {}, {}, {}, {}
    written = []

    def weight_start(j):
        w_own[j].wait()
        w_sib[j].wait_recv()
        gather1[j].start()

    def sibling_tokens():
        f_sib.wait_recv()
        for k in range(PARTS):
            transpose(1, k)

    def take_part(k):
        rows = pl.ds(k * PART, PART)
        f_x[k].wait_recv()
        f_fwd[k] = remote(f.at[2, rows], f.at[3, rows], sib)
        transpose(2, k)

    def take_forwarded(k):
        f_fwd[k].wait_recv()
        transpose(3, k)

    def own_act(j):
        gather1[j].finish()
        matmul(j, v1, a1.at[j], 0, 2)

    def own_delta(j):
        c_own[j].wait()
        c_sib[j].wait_recv()
        delta(j, 0, 2, False)

    def other_delta(j):
        c_x[j].wait_recv()
        delta(j, 2, 4, False)

    def gather_start(j):
        sent(gather1[j].groups)
        gather2[j].start()

    def cross(j):
        scatter1[j].finish()
        swap[j] = remote(t.at[j], tx.at[j], dev(dx=2))

    def first(j):
        swap[j].wait_recv()
        total = t[j].astype(F32) + tx[j].astype(F32)
        v2[j, z, y] = total.astype(BF16)
        sq = (total * total).reshape(2 * ROWS // 8, 8, BLK).sum(axis=0)
        sq = sq[:, :128] + sq[:, 128:]
        nown[0] = sq if j == 0 else nown[0] + sq

    def norm_send(i):
        state[i] = Group(nrecv.at[i])
        for n, device in enumerate(norm_rings[i]):
            state[i].send(nown.at[i], nrecv.at[i, n], device)

    def norm_add(i):
        state[i].wait_recv()
        return nown[i] + nrecv[i, 0] + nrecv[i, 1] + nrecv[i, 2]

    def norm_turn(i):
        nown[i] = norm_add(i - 1)
        norm_send(i)

    def norm_finish():
        total = jnp.sum(norm_add(2), keepdims=True)
        factor = 0.3 * jnp.sqrt(F32(DO)) / jnp.sqrt(total + 1e-06)
        kvec[...] = jnp.broadcast_to(factor, kvec.shape)

    def second_act(j):
        gather2[j].finish()
        matmul(j, v2, a2, 0, 4)

    def second_grad(j):
        sent(scatter1[j].groups)
        grad(j, 0, 4, False)

    def spread(j):
        sent([swap[j]])
        scatter2[j].finish()
        far = Group(o.at[j, 1:4])
        for step in (2, 1, 3):
            far.send(t.at[j, core], o.at[j, step, 0], dev(dx=step))
            far.send(t.at[j, 1 - core], o.at[j, step, 1], dev(dx=step, other=True))
        share[j] = [far, remote(t.at[j, 1 - core], o.at[j, 0, 1], sib)]

    def collect(j):
        for cp in share[j]:
            cp.wait_recv()
        for other in (False, True):
            same = t[j, core] if not other else o[j, 0, 1]
            k = int(other)
            result[j, 0, k] = (same.astype(F32) + o[j, 2, k].astype(F32)).astype(BF16)
            result[j, 1, k] = (o[j, 1, k].astype(F32) + o[j, 3, k].astype(F32)).astype(BF16)
        for parity in (0, 1):
            for k in (0, 1):
                written.append(local(result.at[j, parity, k], out.at[:, columns(parity, k == 1, j)]))

    steps = {
        "aS": weight_start,
        "aT": lambda j: gather1[j].turn(),
        "aG": lambda j: gather1[j].forward(),
        "F": take_part,
        "G": take_forwarded,
        "oA": own_act,
        "oD": own_delta,
        "oG": lambda j: grad(j, 0, 2, False),
        "nA": lambda j: matmul(j, v1, a1.at[j], 2, 4),
        "nD": other_delta,
        "nG": lambda j: grad(j, 2, 4, True),
        "rS": lambda j: scatter1[j].start(),
        "rM": lambda j: scatter1[j].middle(),
        "rT": lambda j: scatter1[j].turn(),
        "rX": cross,
        "rFirst": first,
        "bS": gather_start,
        "bT": lambda j: gather2[j].turn(),
        "bG": lambda j: gather2[j].forward(),
        "pA": second_act,
        "pD": lambda j: delta(j, 0, 4, True),
        "pG": second_grad,
        "qS": lambda j: scatter2[j].start(),
        "qM": lambda j: scatter2[j].middle(),
        "qT": lambda j: scatter2[j].turn(),
        "qP": spread,
        "qC": collect,
    }
    single = {
        "T1": sibling_tokens,
        "N0": lambda: norm_send(0),
        "N1": lambda: norm_turn(1),
        "N2": lambda: norm_turn(2),
        "N3": norm_finish,
    }
    for name in ORDER:
        if name in single:
            single[name]()
        else:
            steps[name[:-1]](int(name[-1]))
    drain()
    for cp in written:
        cp.wait()


def body(features, cotangent, weight):
    return pl.pallas_call(
        kernel,
        out_shape=jax.ShapeDtypeStruct((ROWS, DO), BF16),
        in_specs=[pl.BlockSpec(memory_space=pl.ANY)] * 3,
        out_specs=pl.BlockSpec(memory_space=pl.ANY),
        scratch_shapes=[
            pltpu.VMEM((4, TOK, DI), BF16),
            pltpu.VMEM((DI, 4 * TOK), BF16),
            pltpu.VMEM((NB, 4, TOK, BLK), BF16),
            pltpu.VMEM((NB, 4, TOK, BLK), BF16),
            pltpu.VMEM((NB, RING, RING, 2, ROWS, BLK), BF16),
            pltpu.VMEM((NB, RING, RING, 2, ROWS, BLK), BF16),
            pltpu.VMEM((NB, 4, TOK, BLK), F32),
            pltpu.VMEM((4, TOK, BLK), F32),
            pltpu.VMEM((NB, RING, RING, 2, ROWS, BLK), BF16),
            pltpu.VMEM((NB, 2, 3, RING, ROWS, BLK), BF16),
            pltpu.VMEM((NB, 2, 3, ROWS, BLK), BF16),
            pltpu.VMEM((NB, 2, ROWS, BLK), BF16),
            pltpu.VMEM((NB, 2, ROWS, BLK), BF16),
            pltpu.VMEM((NB, 4, 2, ROWS, BLK), BF16),
            pltpu.VMEM((3, 8, 128), F32),
            pltpu.VMEM((3, 3, 8, 128), F32),
            pltpu.VMEM((8, BLK), F32),
            pltpu.VMEM((NB, 2, 2, ROWS, BLK), BF16),
            pltpu.SemaphoreType.DMA((N_SEMS,)),
            pltpu.SemaphoreType.DMA((N_SEMS,)),
            pltpu.SemaphoreType.DMA((19,)),
        ],
        compiler_params=pltpu.CompilerParams(
            collective_id=0, has_side_effects=True, vmem_limit_bytes=60 * 2**20
        ),
    )(features, cotangent, weight).astype(F32)


def solution(mesh):
    in_specs = (P(("dp", "fsdp"), None), P(("dp", "fsdp"), None), P("fsdp", None))
    out_specs = P("fsdp", None)
    return jax.shard_map(body, mesh=mesh, in_specs=in_specs, out_specs=out_specs, check_vma=False)
```

```python
import jax
import jax.numpy as jnp
from jax import lax
from jax.experimental import pallas as pl
from jax.experimental.pallas import tpu as pltpu
from jax.sharding import PartitionSpec as P

MESH = pl.DeviceIdType.MESH
F32 = jnp.float32
BF16 = jnp.bfloat16

RING = 4
TOK = 384
DI = 3072
DO = 3072
ROWS = 96
BLK = 256
NB = 3
SHARE = BLK * NB
PART = 128
PARTS = TOK // PART
N_SEMS = 46
LOW, HIGH = slice(0, RING // 2), slice(RING // 2, RING)
ROOT = 0.7978845608028654
CUBIC = 0.044715
ORDER = (
    "aS0", "aT0", "aS1", "T1", "aG0", "aS2", "F0", "G0", "aT1", "oA0", "oD0", "oG0", "F1", "aT2", "aG1", "G1",
    "aG2", "F2", "G2", "nA0", "nD0", "nG0", "rS0", "oA1", "oD1", "oG1", "nA1", "nD1", "rM0", "nG1", "rS1",
    "oA2", "oD2", "oG2", "rT0", "rM1", "nA2", "nD2", "nG2", "rS2", "rT1", "rX0", "rM2", "rFirst0", "bS0",
    "rX1", "rT2", "bT0", "rFirst1", "bS1", "rX2", "bG0", "rFirst2", "N0", "bS2", "N1", "bT1", "N2", "pA0",
    "N3", "bT2", "bG1", "pD0", "pG0", "qS0", "bG2", "pA1", "qM0", "pD1", "pG1", "qS1", "pA2", "qT0", "pD2",
    "pG2", "qS2", "qM1", "qP0", "qM2", "qC0", "qT1", "qT2", "qP1", "qP2", "qC1", "qC2",
)


def kernel(
    feat, cot, weight, out,
    f, ft, c, d, v1, v2, a1, a2, g, r1, r2, t, tx, o, nown, nrecv, kvec, result,
    send_sems, recv_sems, local_sems,
):
    x = lax.axis_index("dp")
    ff = lax.axis_index("fsdp")
    z = ff // 8
    y = lax.rem(ff // 2, RING)
    core = lax.rem(ff, 2)
    s = 1 - 2 * core

    def wrap(v):
        return lax.rem(v + 2 * RING, RING)

    def dev(dx=0, dy=0, dz=0, other=False):
        cc = 1 - core if other else core
        return (wrap(x + dx), (wrap(z + dz) * RING + wrap(y + dy)) * 2 + cc)

    def ring_dev(axis, step):
        return dev(dy=step) if axis == "y" else dev(dz=step)

    counter = [0]
    pending = []

    class Group:
        def __init__(self, like, again=None):
            self.like = like
            if again is None:
                self.i = counter[0]
                counter[0] += 1
            else:
                self.i = again.i

        def send(self, src, dst, device):
            if not any(group is self for group in pending):
                pending.append(self)
            pltpu.make_async_remote_copy(
                src_ref=src, dst_ref=dst, send_sem=send_sems.at[self.i], recv_sem=recv_sems.at[self.i],
                device_id=device, device_id_type=MESH,
            ).start()

        def wait_recv(self):
            pltpu.make_async_copy(self.like, self.like, recv_sems.at[self.i]).wait()

        def wait_send(self):
            pltpu.make_async_copy(self.like, self.like, send_sems.at[self.i]).wait()
            pending[:] = [group for group in pending if group is not self]

    def remote(src, dst, device):
        group = Group(dst)
        group.send(src, dst, device)
        return group

    def drain():
        for group in list(pending):
            group.wait_send()

    def sent(groups):
        for group in groups:
            group.wait_send()

    local_counter = [0]

    def local(src, dst):
        i = local_counter[0]
        local_counter[0] += 1
        cp = pltpu.make_async_copy(src, dst, local_sems.at[i])
        cp.start()
        return cp

    def columns(dx, other, j):
        cc = 1 - core if other else core
        start = (lax.rem(x + dx + RING, 2) * 2 + cc) * SHARE + j * BLK
        return pl.ds(pl.multiple_of(start, BLK), BLK)

    def transpose(slot, part):
        @pl.loop(0, DI // BLK)
        def _(i):
            cols = pl.ds(pl.multiple_of(i * BLK, BLK), BLK)
            ft[cols, pl.ds(slot * TOK + part * PART, PART)] = f[slot, pl.ds(part * PART, PART), cols].T

    barrier = pltpu.get_barrier_semaphore()
    norm_first = [dev(other=True), dev(dx=1), dev(dx=1, other=True)]
    norm_rings = (norm_first, [dev(dy=n) for n in (1, 2, 3)], [dev(dz=n) for n in (1, 2, 3)])
    others = [dev(other=True)]
    for step in (1, 2, 3):
        others += [dev(dx=step), dev(dx=step, other=True), dev(dy=step), dev(dz=step)]
    for other in others:
        pl.semaphore_signal(barrier, inc=1, device_id=other, device_id_type=MESH)
    w_own = [local(weight.at[:, columns(0, False, j)], v1.at[j, z, y, core]) for j in range(NB)]
    f_own = local(feat, f.at[0])
    c_own = [local(cot.at[:, columns(0, False, j)], c.at[j, 0]) for j in range(NB)]
    pl.semaphore_wait(barrier, len(others))

    sib = dev(other=True)
    f_x, c_x = [], []

    def send_features(k):
        rows = pl.ds(k * PART, PART)
        f_x.append(remote(feat.at[rows], f.at[2, rows], dev(dx=s)))

    def send_cotangent(j):
        c_x.append(Group(c.at[j, 2:4]))
        c_x[j].send(cot.at[:, columns(1, False, j)], c.at[j, 2], dev(dx=s))
        c_x[j].send(cot.at[:, columns(1, True, j)], c.at[j, 3], dev(dx=s, other=True))

    for k in range(PARTS):
        send_features(k)
    for j in range(NB):
        send_cotangent(j)
    w_sib = [
        remote(weight.at[:, columns(0, True, j)], v1.at[j, z, y, core], sib) for j in range(NB)
    ]
    f_sib = remote(feat, f.at[1], sib)
    c_sib = [remote(cot.at[:, columns(0, True, j)], c.at[j, 1], sib) for j in range(NB)]

    f_own.wait()
    for k in range(PARTS):
        transpose(0, k)

    class Gather:
        def __init__(self, v, j, again=None):
            self.v, self.j = v, j
            likes = (v.at[j, 0, 0:3], v.at[j, 0], v.at[j, 0:2])
            self.groups = [Group(like, again and again.groups[i]) for i, like in enumerate(likes)]
            self.direct, self.early, self.late = self.groups

        def axis(self, half, stage):
            return ("y", "z")[(half + stage + 1) % 2]

        def piece(self, half, stage, step, part=None):
            axis = self.axis(half, stage)
            zz = wrap(z + step) if axis == "z" else z
            yy = wrap(y + step) if axis == "y" else y
            if stage == 1:
                return self.v.at[self.j, zz, yy, half]
            if axis == "z":
                return self.v.at[self.j, zz, part, half]
            return self.v.at[self.j, part, yy, half]

        def start(self):
            for half in (0, 1):
                own, axis = self.piece(half, 1, 0), self.axis(half, 1)
                for n in (1, 3, 2):
                    self.direct.send(own, own, ring_dev(axis, n))

        def turn(self):
            self.direct.wait_recv()
            for group, parts in ((self.early, (LOW, HIGH)), (self.late, (HIGH, LOW))):
                for step, part in zip((1, -1), parts):
                    for half in (0, 1):
                        own = self.piece(half, 2, 0, part)
                        group.send(own, own, ring_dev(self.axis(half, 2), step))

        def forward(self):
            self.early.wait_recv()
            for step, part in ((1, LOW), (-1, HIGH)):
                for half in (0, 1):
                    got = self.piece(half, 2, -step, part)
                    self.late.send(got, got, ring_dev(self.axis(half, 2), step))

        def finish(self):
            self.late.wait_recv()

    class Scatter:
        def __init__(self, j, again=None):
            self.j = j
            likes = (r1.at[j, :, 0], r1.at[j, :, 1:3], r2.at[j])
            self.groups = [Group(like, again and again.groups[i]) for i, like in enumerate(likes)]
            self.far, self.near, self.direct = self.groups

        def axis(self, half, stage):
            return ("z", "y")[(half + stage + 1) % 2]

        def place(self, half, stage, step, part=slice(None)):
            axis = self.axis(half, stage)
            zz = wrap(z + step) if axis == "z" else z
            yy = wrap(y + step) if axis == "y" else y
            if stage == 2:
                return (self.j, zz, yy, half)
            if axis == "z":
                return (self.j, zz, part, half)
            return (self.j, part, yy, half)

        def send(self, group, half, step, to, part, land):
            group.send(
                g.at[self.place(half, 1, step, part)], r1.at[self.j, half, land, part], ring_dev(self.axis(half, 1), to)
            )

        def start(self):
            for step, part in ((1, LOW), (-1, HIGH)):
                for half in (0, 1):
                    self.send(self.far, half, 2, step, part, 0)
            for step, part, land in ((1, HIGH, 1), (-1, LOW, 2)):
                for half in (0, 1):
                    self.send(self.near, half, step, step, part, land)

        def middle(self):
            self.far.wait_recv()
            for step, part, land in ((1, LOW, 1), (-1, HIGH, 2)):
                for half in (0, 1):
                    at = self.place(half, 1, step, part)
                    g[at] = (g[at].astype(F32) + r1[self.j, half, 0, part].astype(F32)).astype(BF16)
                    self.send(self.near, half, step, step, part, land)

        def turn(self):
            self.near.wait_recv()
            for half in (0, 1):
                at = self.place(half, 1, 0)
                total = g[at].astype(F32) + r1[self.j, half, 1].astype(F32) + r1[self.j, half, 2].astype(F32)
                g[at] = total.astype(BF16)
                for n in (1, 3, 2):
                    self.direct.send(
                        g.at[self.place(half, 2, n)], r2.at[self.j, half, n - 1], ring_dev(self.axis(half, 2), n)
                    )

        def finish(self):
            self.direct.wait_recv()
            for half in (0, 1):
                total = g[self.place(half, 2, 0)].astype(F32)
                for n in range(3):
                    total = total + r2[self.j, half, n].astype(F32)
                t[self.j, half] = total.astype(BF16)

    def matmul(j, v, dst, lo, hi):
        @pl.loop(lo, hi)
        def _(slot):
            dst[slot] = jnp.dot(f[slot], v[j].reshape(DI, BLK), preferred_element_type=F32)

    def delta(j, lo, hi, second):
        step = 64

        @pl.loop(lo, hi)
        def _(slot):
            @pl.loop(0, TOK // step)
            def _(i):
                rows = pl.ds(pl.multiple_of(i * step, step), step)
                a = a1[j, slot, rows, :]
                if second:
                    a = a + a2[slot, rows, :] * kvec[0:1, :]
                square = a * a
                th = jnp.tanh(ROOT * a * (1.0 + CUBIC * square))
                slope = 0.5 * (1.0 + th) + 0.5 * a * (1.0 - th * th) * (ROOT * (1.0 + 3.0 * CUBIC * square))
                scaled = c[j, slot, rows, :].astype(F32) * (1.0 / jnp.sqrt(F32(TOK * 128)))
                d[j, slot, rows, :] = (scaled * slope).astype(BF16)

    def grad(j, lo, hi, add):
        rows = DI // 4

        @pl.loop(0, 4)
        def _(i):
            left = ft[pl.ds(pl.multiple_of(i * rows, rows), rows), lo * TOK : hi * TOK]
            right = d[j, lo:hi].reshape((hi - lo) * TOK, BLK)
            term = jnp.dot(left, right, preferred_element_type=F32)
            at = (j, pl.ds(i, 1))
            if add:
                term = term + g[at].reshape(rows, BLK).astype(F32)
            g[at] = term.astype(BF16).reshape(1, RING, 2, ROWS, BLK)

    gather1 = [Gather(v1, j) for j in range(NB)]
    gather2 = [Gather(v2, j, gather1[j]) for j in range(NB)]
    scatter1 = [Scatter(j) for j in range(NB)]
    scatter2 = [Scatter(j, scatter1[j]) for j in range(NB)]
    f_fwd, swap, share, state = {}, {}, {}, {}
    written = []

    def weight_start(j):
        w_own[j].wait()
        w_sib[j].wait_recv()
        gather1[j].start()

    def sibling_tokens():
        f_sib.wait_recv()
        for k in range(PARTS):
            transpose(1, k)

    def take_part(k):
        rows = pl.ds(k * PART, PART)
        f_x[k].wait_recv()
        f_fwd[k] = remote(f.at[2, rows], f.at[3, rows], sib)
        transpose(2, k)

    def take_forwarded(k):
        f_fwd[k].wait_recv()
        transpose(3, k)

    def own_act(j):
        gather1[j].finish()
        matmul(j, v1, a1.at[j], 0, 2)

    def own_delta(j):
        c_own[j].wait()
        c_sib[j].wait_recv()
        delta(j, 0, 2, False)

    def other_delta(j):
        c_x[j].wait_recv()
        delta(j, 2, 4, False)

    def gather_start(j):
        sent(gather1[j].groups)
        gather2[j].start()

    def cross(j):
        scatter1[j].finish()
        swap[j] = remote(t.at[j], tx.at[j], dev(dx=2))

    def first(j):
        swap[j].wait_recv()
        total = t[j].astype(F32) + tx[j].astype(F32)
        v2[j, z, y] = total.astype(BF16)
        sq = (total * total).reshape(2 * ROWS // 8, 8, BLK).sum(axis=0)
        sq = sq[:, :128] + sq[:, 128:]
        nown[0] = sq if j == 0 else nown[0] + sq

    def norm_send(i):
        state[i] = Group(nrecv.at[i])
        for n, device in enumerate(norm_rings[i]):
            state[i].send(nown.at[i], nrecv.at[i, n], device)

    def norm_add(i):
        state[i].wait_recv()
        return nown[i] + nrecv[i, 0] + nrecv[i, 1] + nrecv[i, 2]

    def norm_turn(i):
        nown[i] = norm_add(i - 1)
        norm_send(i)

    def norm_finish():
        total = jnp.sum(norm_add(2), keepdims=True)
        factor = 0.3 * jnp.sqrt(F32(DO)) / jnp.sqrt(total + 1e-06)
        kvec[...] = jnp.broadcast_to(factor, kvec.shape)

    def second_act(j):
        gather2[j].finish()
        matmul(j, v2, a2, 0, 4)

    def second_grad(j):
        sent(scatter1[j].groups)
        grad(j, 0, 4, False)

    def spread(j):
        sent([swap[j]])
        scatter2[j].finish()
        far = Group(o.at[j, 1:4])
        for step in (2, 1, 3):
            far.send(t.at[j, core], o.at[j, step, 0], dev(dx=step))
            far.send(t.at[j, 1 - core], o.at[j, step, 1], dev(dx=step, other=True))
        share[j] = [far, remote(t.at[j, 1 - core], o.at[j, 0, 1], sib)]

    def collect(j):
        for cp in share[j]:
            cp.wait_recv()
        for other in (False, True):
            same = t[j, core] if not other else o[j, 0, 1]
            k = int(other)
            result[j, 0, k] = (same.astype(F32) + o[j, 2, k].astype(F32)).astype(BF16)
            result[j, 1, k] = (o[j, 1, k].astype(F32) + o[j, 3, k].astype(F32)).astype(BF16)
        for parity in (0, 1):
            for k in (0, 1):
                written.append(local(result.at[j, parity, k], out.at[:, columns(parity, k == 1, j)]))

    steps = {
        "aS": weight_start,
        "aT": lambda j: gather1[j].turn(),
        "aG": lambda j: gather1[j].forward(),
        "F": take_part,
        "G": take_forwarded,
        "oA": own_act,
        "oD": own_delta,
        "oG": lambda j: grad(j, 0, 2, False),
        "nA": lambda j: matmul(j, v1, a1.at[j], 2, 4),
        "nD": other_delta,
        "nG": lambda j: grad(j, 2, 4, True),
        "rS": lambda j: scatter1[j].start(),
        "rM": lambda j: scatter1[j].middle(),
        "rT": lambda j: scatter1[j].turn(),
        "rX": cross,
        "rFirst": first,
        "bS": gather_start,
        "bT": lambda j: gather2[j].turn(),
        "bG": lambda j: gather2[j].forward(),
        "pA": second_act,
        "pD": lambda j: delta(j, 0, 4, True),
        "pG": second_grad,
        "qS": lambda j: scatter2[j].start(),
        "qM": lambda j: scatter2[j].middle(),
        "qT": lambda j: scatter2[j].turn(),
        "qP": spread,
        "qC": collect,
    }
    single = {
        "T1": sibling_tokens,
        "N0": lambda: norm_send(0),
        "N1": lambda: norm_turn(1),
        "N2": lambda: norm_turn(2),
        "N3": norm_finish,
    }
    for name in ORDER:
        if name in single:
            single[name]()
        else:
            steps[name[:-1]](int(name[-1]))
    drain()
    for cp in written:
        cp.wait()


def body(features, cotangent, weight):
    return pl.pallas_call(
        kernel,
        out_shape=jax.ShapeDtypeStruct((ROWS, DO), BF16),
        in_specs=[pl.BlockSpec(memory_space=pl.ANY)] * 3,
        out_specs=pl.BlockSpec(memory_space=pl.ANY),
        scratch_shapes=[
            pltpu.VMEM((4, TOK, DI), BF16),
            pltpu.VMEM((DI, 4 * TOK), BF16),
            pltpu.VMEM((NB, 4, TOK, BLK), BF16),
            pltpu.VMEM((NB, 4, TOK, BLK), BF16),
            pltpu.VMEM((NB, RING, RING, 2, ROWS, BLK), BF16),
            pltpu.VMEM((NB, RING, RING, 2, ROWS, BLK), BF16),
            pltpu.VMEM((NB, 4, TOK, BLK), F32),
            pltpu.VMEM((4, TOK, BLK), F32),
            pltpu.VMEM((NB, RING, RING, 2, ROWS, BLK), BF16),
            pltpu.VMEM((NB, 2, 3, RING, ROWS, BLK), BF16),
            pltpu.VMEM((NB, 2, 3, ROWS, BLK), BF16),
            pltpu.VMEM((NB, 2, ROWS, BLK), BF16),
            pltpu.VMEM((NB, 2, ROWS, BLK), BF16),
            pltpu.VMEM((NB, 4, 2, ROWS, BLK), BF16),
            pltpu.VMEM((3, 8, 128), F32),
            pltpu.VMEM((3, 3, 8, 128), F32),
            pltpu.VMEM((8, BLK), F32),
            pltpu.VMEM((NB, 2, 2, ROWS, BLK), BF16),
            pltpu.SemaphoreType.DMA((N_SEMS,)),
            pltpu.SemaphoreType.DMA((N_SEMS,)),
            pltpu.SemaphoreType.DMA((19,)),
        ],
        compiler_params=pltpu.CompilerParams(
            collective_id=0, has_side_effects=True, vmem_limit_bytes=60 * 2**20
        ),
    )(features, cotangent, weight).astype(F32)


def solution(mesh):
    in_specs = (P(("dp", "fsdp"), None), P(("dp", "fsdp"), None), P("fsdp", None))
    out_specs = P("fsdp", None)
    return jax.shard_map(body, mesh=mesh, in_specs=in_specs, out_specs=out_specs, check_vma=False)
```

```python
import jax
import jax.numpy as jnp
from jax import lax
from jax.experimental import pallas as pl
from jax.experimental.pallas import tpu as pltpu
from jax.sharding import PartitionSpec as P

MESH = pl.DeviceIdType.MESH
F32 = jnp.float32
BF16 = jnp.bfloat16

RING = 4
TOK = 384
DI = 3072
DO = 3072
ROWS = 96
BLK = 256
NB = 3
SHARE = BLK * NB
PART = 128
PARTS = TOK // PART
N_SEMS = 46
LOW, HIGH = slice(0, RING // 2), slice(RING // 2, RING)
ROOT = 0.7978845608028654
CUBIC = 0.044715
ORDER = (
    "aS0", "aT0", "aS1", "T1", "aG0", "aS2", "F0", "G0", "aT1", "oA0", "oD0", "oG0", "F1", "aT2", "aG1", "G1",
    "aG2", "F2", "G2", "nA0", "nD0", "nG0", "rS0", "oA1", "oD1", "oG1", "rM0", "nA1", "nD1", "nG1", "rS1",
    "oA2", "oD2", "oG2", "rT0", "rM1", "nA2", "nD2", "nG2", "rS2", "rX0", "rT1", "rM2", "rFirst0", "bS0",
    "rX1", "rT2", "bT0", "rFirst1", "bS1", "rX2", "bG0", "rFirst2", "N0", "bS2", "N1", "bT1", "N2", "pA0",
    "N3", "bT2", "bG1", "pD0", "pG0", "qS0", "bG2", "pA1", "qM0", "pD1", "pG1", "qS1", "pA2", "qT0", "pD2",
    "pG2", "qS2", "qM1", "qP0", "qM2", "qC0", "qT1", "qT2", "qP1", "qP2", "qC1", "qC2",
)


def kernel(
    feat, cot, weight, out,
    f, ft, c, d, v1, v2, a1, a2, g, r1, r2, t, tx, o, nown, nrecv, kvec, result,
    send_sems, recv_sems, local_sems,
):
    x = lax.axis_index("dp")
    ff = lax.axis_index("fsdp")
    z = ff // 8
    y = lax.rem(ff // 2, RING)
    core = lax.rem(ff, 2)
    s = 1 - 2 * core

    def wrap(v):
        return lax.rem(v + 2 * RING, RING)

    def dev(dx=0, dy=0, dz=0, other=False):
        cc = 1 - core if other else core
        return (wrap(x + dx), (wrap(z + dz) * RING + wrap(y + dy)) * 2 + cc)

    def ring_dev(axis, step):
        return dev(dy=step) if axis == "y" else dev(dz=step)

    counter = [0]
    pending = []

    class Group:
        def __init__(self, like, again=None):
            self.like = like
            if again is None:
                self.i = counter[0]
                counter[0] += 1
            else:
                self.i = again.i

        def send(self, src, dst, device):
            if not any(group is self for group in pending):
                pending.append(self)
            pltpu.make_async_remote_copy(
                src_ref=src, dst_ref=dst, send_sem=send_sems.at[self.i], recv_sem=recv_sems.at[self.i],
                device_id=device, device_id_type=MESH,
            ).start()

        def wait_recv(self):
            pltpu.make_async_copy(self.like, self.like, recv_sems.at[self.i]).wait()

        def wait_send(self):
            pltpu.make_async_copy(self.like, self.like, send_sems.at[self.i]).wait()
            pending[:] = [group for group in pending if group is not self]

    def remote(src, dst, device):
        group = Group(dst)
        group.send(src, dst, device)
        return group

    def drain():
        for group in list(pending):
            group.wait_send()

    def sent(groups):
        for group in groups:
            group.wait_send()

    local_counter = [0]

    def local(src, dst):
        i = local_counter[0]
        local_counter[0] += 1
        cp = pltpu.make_async_copy(src, dst, local_sems.at[i])
        cp.start()
        return cp

    def columns(dx, other, j):
        cc = 1 - core if other else core
        start = (lax.rem(x + dx + RING, 2) * 2 + cc) * SHARE + j * BLK
        return pl.ds(pl.multiple_of(start, BLK), BLK)

    def transpose(slot, part):
        @pl.loop(0, DI // BLK)
        def _(i):
            cols = pl.ds(pl.multiple_of(i * BLK, BLK), BLK)
            ft[cols, pl.ds(slot * TOK + part * PART, PART)] = f[slot, pl.ds(part * PART, PART), cols].T

    barrier = pltpu.get_barrier_semaphore()
    norm_first = [dev(other=True), dev(dx=1), dev(dx=1, other=True)]
    norm_rings = (norm_first, [dev(dy=n) for n in (1, 2, 3)], [dev(dz=n) for n in (1, 2, 3)])
    others = [dev(other=True)]
    for step in (1, 2, 3):
        others += [dev(dx=step), dev(dx=step, other=True), dev(dy=step), dev(dz=step)]
    for other in others:
        pl.semaphore_signal(barrier, inc=1, device_id=other, device_id_type=MESH)
    w_own = [local(weight.at[:, columns(0, False, j)], v1.at[j, z, y, core]) for j in range(NB)]
    f_own = local(feat, f.at[0])
    c_own = [local(cot.at[:, columns(0, False, j)], c.at[j, 0]) for j in range(NB)]
    pl.semaphore_wait(barrier, len(others))

    sib = dev(other=True)
    f_x, c_x = [], []

    def send_features(k):
        rows = pl.ds(k * PART, PART)
        f_x.append(remote(feat.at[rows], f.at[2, rows], dev(dx=s)))

    def send_cotangent(j):
        c_x.append(Group(c.at[j, 2:4]))
        c_x[j].send(cot.at[:, columns(1, False, j)], c.at[j, 2], dev(dx=s))
        c_x[j].send(cot.at[:, columns(1, True, j)], c.at[j, 3], dev(dx=s, other=True))

    for k in range(PARTS):
        send_features(k)
    for j in range(NB):
        send_cotangent(j)
    w_sib = [
        remote(weight.at[:, columns(0, True, j)], v1.at[j, z, y, core], sib) for j in range(NB)
    ]
    f_sib = remote(feat, f.at[1], sib)
    c_sib = [remote(cot.at[:, columns(0, True, j)], c.at[j, 1], sib) for j in range(NB)]

    f_own.wait()
    for k in range(PARTS):
        transpose(0, k)

    class Gather:
        def __init__(self, v, j, again=None):
            self.v, self.j = v, j
            likes = (v.at[j, 0, 0:3], v.at[j, 0], v.at[j, 0:2])
            self.groups = [Group(like, again and again.groups[i]) for i, like in enumerate(likes)]
            self.direct, self.early, self.late = self.groups

        def axis(self, half, stage):
            return ("y", "z")[(half + stage + 1) % 2]

        def piece(self, half, stage, step, part=None):
            axis = self.axis(half, stage)
            zz = wrap(z + step) if axis == "z" else z
            yy = wrap(y + step) if axis == "y" else y
            if stage == 1:
                return self.v.at[self.j, zz, yy, half]
            if axis == "z":
                return self.v.at[self.j, zz, part, half]
            return self.v.at[self.j, part, yy, half]

        def start(self):
            for half in (0, 1):
                own, axis = self.piece(half, 1, 0), self.axis(half, 1)
                for n in (1, 3, 2):
                    self.direct.send(own, own, ring_dev(axis, n))

        def turn(self):
            self.direct.wait_recv()
            for group, parts in ((self.early, (LOW, HIGH)), (self.late, (HIGH, LOW))):
                for step, part in zip((1, -1), parts):
                    for half in (0, 1):
                        own = self.piece(half, 2, 0, part)
                        group.send(own, own, ring_dev(self.axis(half, 2), step))

        def forward(self):
            self.early.wait_recv()
            for step, part in ((1, LOW), (-1, HIGH)):
                for half in (0, 1):
                    got = self.piece(half, 2, -step, part)
                    self.late.send(got, got, ring_dev(self.axis(half, 2), step))

        def finish(self):
            self.late.wait_recv()

    class Scatter:
        def __init__(self, j, again=None):
            self.j = j
            likes = (r1.at[j, :, 0], r1.at[j, :, 1:3], r2.at[j])
            self.groups = [Group(like, again and again.groups[i]) for i, like in enumerate(likes)]
            self.far, self.near, self.direct = self.groups

        def axis(self, half, stage):
            return ("z", "y")[(half + stage + 1) % 2]

        def place(self, half, stage, step, part=slice(None)):
            axis = self.axis(half, stage)
            zz = wrap(z + step) if axis == "z" else z
            yy = wrap(y + step) if axis == "y" else y
            if stage == 2:
                return (self.j, zz, yy, half)
            if axis == "z":
                return (self.j, zz, part, half)
            return (self.j, part, yy, half)

        def send(self, group, half, step, to, part, land):
            group.send(
                g.at[self.place(half, 1, step, part)], r1.at[self.j, half, land, part], ring_dev(self.axis(half, 1), to)
            )

        def start(self):
            for step, part in ((1, LOW), (-1, HIGH)):
                for half in (0, 1):
                    self.send(self.far, half, 2, step, part, 0)
            for step, part, land in ((1, HIGH, 1), (-1, LOW, 2)):
                for half in (0, 1):
                    self.send(self.near, half, step, step, part, land)

        def middle(self):
            self.far.wait_recv()
            for step, part, land in ((1, LOW, 1), (-1, HIGH, 2)):
                for half in (0, 1):
                    at = self.place(half, 1, step, part)
                    g[at] = (g[at].astype(F32) + r1[self.j, half, 0, part].astype(F32)).astype(BF16)
                    self.send(self.near, half, step, step, part, land)

        def turn(self):
            self.near.wait_recv()
            for half in (0, 1):
                at = self.place(half, 1, 0)
                total = g[at].astype(F32) + r1[self.j, half, 1].astype(F32) + r1[self.j, half, 2].astype(F32)
                g[at] = total.astype(BF16)
                for n in (1, 3, 2):
                    self.direct.send(
                        g.at[self.place(half, 2, n)], r2.at[self.j, half, n - 1], ring_dev(self.axis(half, 2), n)
                    )

        def finish(self):
            self.direct.wait_recv()
            for half in (0, 1):
                total = g[self.place(half, 2, 0)].astype(F32)
                for n in range(3):
                    total = total + r2[self.j, half, n].astype(F32)
                t[self.j, half] = total.astype(BF16)

    def matmul(j, v, dst, lo, hi):
        @pl.loop(lo, hi)
        def _(slot):
            dst[slot] = jnp.dot(f[slot], v[j].reshape(DI, BLK), preferred_element_type=F32)

    def delta(j, lo, hi, second):
        step = 64

        @pl.loop(lo, hi)
        def _(slot):
            @pl.loop(0, TOK // step)
            def _(i):
                rows = pl.ds(pl.multiple_of(i * step, step), step)
                a = a1[j, slot, rows, :]
                if second:
                    a = a + a2[slot, rows, :] * kvec[0:1, :]
                square = a * a
                th = jnp.tanh(ROOT * a * (1.0 + CUBIC * square))
                slope = 0.5 * (1.0 + th) + 0.5 * a * (1.0 - th * th) * (ROOT * (1.0 + 3.0 * CUBIC * square))
                scaled = c[j, slot, rows, :].astype(F32) * (1.0 / jnp.sqrt(F32(TOK * 128)))
                d[j, slot, rows, :] = (scaled * slope).astype(BF16)

    def grad(j, lo, hi, add):
        rows = DI // 4

        @pl.loop(0, 4)
        def _(i):
            left = ft[pl.ds(pl.multiple_of(i * rows, rows), rows), lo * TOK : hi * TOK]
            right = d[j, lo:hi].reshape((hi - lo) * TOK, BLK)
            term = jnp.dot(left, right, preferred_element_type=F32)
            at = (j, pl.ds(i, 1))
            if add:
                term = term + g[at].reshape(rows, BLK).astype(F32)
            g[at] = term.astype(BF16).reshape(1, RING, 2, ROWS, BLK)

    gather1 = [Gather(v1, j) for j in range(NB)]
    gather2 = [Gather(v2, j, gather1[j]) for j in range(NB)]
    scatter1 = [Scatter(j) for j in range(NB)]
    scatter2 = [Scatter(j, scatter1[j]) for j in range(NB)]
    f_fwd, swap, share, state = {}, {}, {}, {}
    written = []

    def weight_start(j):
        w_own[j].wait()
        w_sib[j].wait_recv()
        gather1[j].start()

    def sibling_tokens():
        f_sib.wait_recv()
        for k in range(PARTS):
            transpose(1, k)

    def take_part(k):
        rows = pl.ds(k * PART, PART)
        f_x[k].wait_recv()
        f_fwd[k] = remote(f.at[2, rows], f.at[3, rows], sib)
        transpose(2, k)

    def take_forwarded(k):
        f_fwd[k].wait_recv()
        transpose(3, k)

    def own_act(j):
        gather1[j].finish()
        matmul(j, v1, a1.at[j], 0, 2)

    def own_delta(j):
        c_own[j].wait()
        c_sib[j].wait_recv()
        delta(j, 0, 2, False)

    def other_delta(j):
        c_x[j].wait_recv()
        delta(j, 2, 4, False)

    def gather_start(j):
        sent(gather1[j].groups)
        gather2[j].start()

    def cross(j):
        scatter1[j].finish()
        swap[j] = remote(t.at[j], tx.at[j], dev(dx=2))

    def first(j):
        swap[j].wait_recv()
        total = t[j].astype(F32) + tx[j].astype(F32)
        v2[j, z, y] = total.astype(BF16)
        sq = (total * total).reshape(2 * ROWS // 8, 8, BLK).sum(axis=0)
        sq = sq[:, :128] + sq[:, 128:]
        nown[0] = sq if j == 0 else nown[0] + sq

    def norm_send(i):
        state[i] = Group(nrecv.at[i])
        for n, device in enumerate(norm_rings[i]):
            state[i].send(nown.at[i], nrecv.at[i, n], device)

    def norm_add(i):
        state[i].wait_recv()
        return nown[i] + nrecv[i, 0] + nrecv[i, 1] + nrecv[i, 2]

    def norm_turn(i):
        nown[i] = norm_add(i - 1)
        norm_send(i)

    def norm_finish():
        total = jnp.sum(norm_add(2), keepdims=True)
        factor = 0.3 * jnp.sqrt(F32(DO)) / jnp.sqrt(total + 1e-06)
        kvec[...] = jnp.broadcast_to(factor, kvec.shape)

    def second_act(j):
        gather2[j].finish()
        matmul(j, v2, a2, 0, 4)

    def second_grad(j):
        sent(scatter1[j].groups)
        grad(j, 0, 4, False)

    def spread(j):
        sent([swap[j]])
        scatter2[j].finish()
        far = Group(o.at[j, 1:4])
        for step in (2, 1, 3):
            far.send(t.at[j, core], o.at[j, step, 0], dev(dx=step))
            far.send(t.at[j, 1 - core], o.at[j, step, 1], dev(dx=step, other=True))
        share[j] = [far, remote(t.at[j, 1 - core], o.at[j, 0, 1], sib)]

    def collect(j):
        for cp in share[j]:
            cp.wait_recv()
        for other in (False, True):
            same = t[j, core] if not other else o[j, 0, 1]
            k = int(other)
            result[j, 0, k] = (same.astype(F32) + o[j, 2, k].astype(F32)).astype(BF16)
            result[j, 1, k] = (o[j, 1, k].astype(F32) + o[j, 3, k].astype(F32)).astype(BF16)
        for parity in (0, 1):
            for k in (0, 1):
                written.append(local(result.at[j, parity, k], out.at[:, columns(parity, k == 1, j)]))

    steps = {
        "aS": weight_start,
        "aT": lambda j: gather1[j].turn(),
        "aG": lambda j: gather1[j].forward(),
        "F": take_part,
        "G": take_forwarded,
        "oA": own_act,
        "oD": own_delta,
        "oG": lambda j: grad(j, 0, 2, False),
        "nA": lambda j: matmul(j, v1, a1.at[j], 2, 4),
        "nD": other_delta,
        "nG": lambda j: grad(j, 2, 4, True),
        "rS": lambda j: scatter1[j].start(),
        "rM": lambda j: scatter1[j].middle(),
        "rT": lambda j: scatter1[j].turn(),
        "rX": cross,
        "rFirst": first,
        "bS": gather_start,
        "bT": lambda j: gather2[j].turn(),
        "bG": lambda j: gather2[j].forward(),
        "pA": second_act,
        "pD": lambda j: delta(j, 0, 4, True),
        "pG": second_grad,
        "qS": lambda j: scatter2[j].start(),
        "qM": lambda j: scatter2[j].middle(),
        "qT": lambda j: scatter2[j].turn(),
        "qP": spread,
        "qC": collect,
    }
    single = {
        "T1": sibling_tokens,
        "N0": lambda: norm_send(0),
        "N1": lambda: norm_turn(1),
        "N2": lambda: norm_turn(2),
        "N3": norm_finish,
    }
    for name in ORDER:
        if name in single:
            single[name]()
        else:
            steps[name[:-1]](int(name[-1]))
    drain()
    for cp in written:
        cp.wait()


def body(features, cotangent, weight):
    return pl.pallas_call(
        kernel,
        out_shape=jax.ShapeDtypeStruct((ROWS, DO), BF16),
        in_specs=[pl.BlockSpec(memory_space=pl.ANY)] * 3,
        out_specs=pl.BlockSpec(memory_space=pl.ANY),
        scratch_shapes=[
            pltpu.VMEM((4, TOK, DI), BF16),
            pltpu.VMEM((DI, 4 * TOK), BF16),
            pltpu.VMEM((NB, 4, TOK, BLK), BF16),
            pltpu.VMEM((NB, 4, TOK, BLK), BF16),
            pltpu.VMEM((NB, RING, RING, 2, ROWS, BLK), BF16),
            pltpu.VMEM((NB, RING, RING, 2, ROWS, BLK), BF16),
            pltpu.VMEM((NB, 4, TOK, BLK), F32),
            pltpu.VMEM((4, TOK, BLK), F32),
            pltpu.VMEM((NB, RING, RING, 2, ROWS, BLK), BF16),
            pltpu.VMEM((NB, 2, 3, RING, ROWS, BLK), BF16),
            pltpu.VMEM((NB, 2, 3, ROWS, BLK), BF16),
            pltpu.VMEM((NB, 2, ROWS, BLK), BF16),
            pltpu.VMEM((NB, 2, ROWS, BLK), BF16),
            pltpu.VMEM((NB, 4, 2, ROWS, BLK), BF16),
            pltpu.VMEM((3, 8, 128), F32),
            pltpu.VMEM((3, 3, 8, 128), F32),
            pltpu.VMEM((8, BLK), F32),
            pltpu.VMEM((NB, 2, 2, ROWS, BLK), BF16),
            pltpu.SemaphoreType.DMA((N_SEMS,)),
            pltpu.SemaphoreType.DMA((N_SEMS,)),
            pltpu.SemaphoreType.DMA((19,)),
        ],
        compiler_params=pltpu.CompilerParams(
            collective_id=0, has_side_effects=True, vmem_limit_bytes=60 * 2**20
        ),
    )(features, cotangent, weight).astype(F32)


def solution(mesh):
    in_specs = (P(("dp", "fsdp"), None), P(("dp", "fsdp"), None), P("fsdp", None))
    out_specs = P("fsdp", None)
    return jax.shard_map(body, mesh=mesh, in_specs=in_specs, out_specs=out_specs, check_vma=False)
```
